768 devices in a mesh: replica: 32 (over y, x), tok: 24 (over z, core).
Axes of the slice: x: 4, y: 8, z: 12, core: 2. Of those that a mesh axis runs over, the one named last changes fastest.
Arguments:
- activations: bfloat16 [196608, 2880], P(('replica', 'tok')), may hold values from -24 to 24
- cotangent: bfloat16 [196608, 512], P(('replica', 'tok')), may hold values from -6 to 6
- next_inputs: bfloat16 [196608, 2880], P(('replica', 'tok')), may hold values from -6 to 6
- weight_tiles: bfloat16 [360, 4096], P('tok'), may hold values from -0.109375 to 0.109375
- momentum: float32 [32, 360, 4096], P('replica', 'tok'), may hold values from -6 to 6
- chosen: int32 [32, 24, 8], P('replica', 'tok'), may hold values from 0 to 14, as said below
- counts: int32 [32, 24], P('replica', 'tok'), may hold values from 1 to 8, as said below
Outputs:
- values: bfloat16 [196608, 512], P(('replica', 'tok'))
- new_momentum: float32 [32, 360, 4096], P('replica', 'tok')
The draws below stay inside these ranges and needn't reach their ends.
Inputs may be any that keep to these rules, and one draw needn't show every extreme that they name: Each list chosen[r, k] names 8 different tile numbers of the shard's 15 tiles; only the first counts[r, k] of them are selected. `counts`: in every draw some token shard has 8 selected tiles in every replica.
All inputs are finite; a program needn't handle non-finite values.
Results may differ from the reference program's by a relative error of at most 0.015.
Values may be sent and summed in bfloat16 or wider, within the bound.
A program may use at most 64 MiB of HBM per device.

```python
import math
import jax
import jax.numpy as jnp
from jax import lax

D = 2880
KV = 512
TOK_DEV = 256
TILE = 64
KEEP = 32
SLOTS = 8
REPLICAS = 32
TOK_SHARDS = 24
ROWS_REP = 6144
ROWS_ALL = 196608
TILES = 360
TILES_DEV = 15


def draw_chosen(key, part):
    scores = jax.random.randint(jax.random.fold_in(key, 11), (REPLICAS, TOK_SHARDS, TILES_DEV), 0, 1 << 20)
    scores = scores * TILES_DEV + jnp.arange(TILES_DEV, dtype=jnp.int32)
    order = jnp.argsort(scores, axis=-1)
    return order[:, :, :SLOTS].astype(jnp.int32)


def draw_counts(key, part):
    spread = jax.random.randint(jax.random.fold_in(key, 23), (REPLICAS, TOK_SHARDS), 1, SLOTS + 1)
    busiest = jax.random.randint(jax.random.fold_in(key, 29), (), 0, TOK_SHARDS)
    filled = jnp.arange(TOK_SHARDS, dtype=jnp.int32)[None, :] == busiest
    return jnp.where(filled, SLOTS, spread).astype(jnp.int32)


def strengthened(values, rng, source, target, blocks, factor):
    def block_of(axis_at):
        return (jnp.arange(values.shape[axis_at]) // (values.shape[axis_at] // blocks)).reshape((-1,) + (1,) * (values.ndim - 1 - axis_at))

    near = jax.random.permutation(rng, blocks)[block_of(target)]
    far = (block_of(target) + blocks // 2) % blocks
    return jnp.where((block_of(source) == near) | (block_of(source) == far), factor * values, values)


def block_levels(own_key, shape, split, low, top_value):
    loudness = 1.0
    for dim, parts in split:
        heights = jax.random.uniform(jax.random.fold_in(jax.random.fold_in(own_key, 6), dim), (parts,), jnp.float32, low / len(split), top_value / len(split))
        loudness = loudness * jnp.repeat(jnp.exp(heights), shape[dim] // parts).reshape((-1,) + (1,) * (len(shape) - 1 - dim))
    return loudness


def scatter_about(own_key, dims, width, bound, split=(), held_as=jnp.bfloat16):
    factor_of = block_levels(own_key, dims, split, -0.22, 0.18) if split else 1.0
    array = jax.random.normal(own_key, dims, jnp.float32) * width * factor_of
    return jnp.minimum(jnp.maximum(array, -bound), bound).astype(held_as)


def heavy_noise(key, extent, scale, reach, shards, heavy, kind=jnp.bfloat16):
    result = scale * jax.random.normal(key, extent, jnp.float32)
    if shards:
        result = result * block_levels(key, extent, shards, -0.22, 0.18)
    return jnp.clip(strengthened(result, jax.random.fold_in(key, 3), *heavy), -reach, reach).astype(kind)


def setup_inputs(seed: int = 0) -> dict:
    seeds = jax.random.split(jax.random.key(seed), 8)
    activations = heavy_noise(seeds[0], (ROWS_ALL, D), 1.0, 24.0, ((0, 768),), (0, 1, 192, 6.0))
    cotangent = scatter_about(seeds[1], (ROWS_ALL, KV), 1.0, 6.0, ((0, 768),))
    next_inputs = scatter_about(seeds[2], (ROWS_ALL, D), 1.0, 6.0, ((0, 768),))
    weight_tiles = scatter_about(seeds[3], (TILES, TILE * TILE), D ** -0.5, 0.109375, ((0, 24),))
    momentum = scatter_about(seeds[4], (REPLICAS, TILES, TILE * TILE), 1.0, 6.0, ((0, 32), (1, 24)), jnp.float32)
    chosen = draw_chosen(jax.random.fold_in(seeds[7], 71), 0)
    counts = draw_counts(jax.random.fold_in(seeds[7], 71), 0)
    return dict(activations=activations, cotangent=cotangent, next_inputs=next_inputs, weight_tiles=weight_tiles, momentum=momentum, chosen=chosen, counts=counts)


momentum_decay = 0.9
step_size = 0.01

def cosine_rows(count):
    frequency = jnp.arange(count, dtype=jnp.float32)[:, None]
    position = jnp.arange(TILE, dtype=jnp.float32)[None, :]
    cosines = jnp.cos(math.pi * (2.0 * position + 1.0) * frequency / (2.0 * TILE))
    factor = jnp.where(frequency == 0, math.sqrt(1.0 / TILE), math.sqrt(2.0 / TILE))
    return (cosines * factor).astype(jnp.float32)

def to_tiles(matrix):
    row_tiles = matrix.shape[0] // TILE
    col_tiles = matrix.shape[1] // TILE
    shaped = matrix.reshape(row_tiles, TILE, col_tiles, TILE).transpose(0, 2, 1, 3)
    return shaped.reshape(row_tiles * col_tiles, TILE * TILE)

def from_tiles(tiled):
    shaped = tiled.reshape(D // TILE, KV // TILE, TILE, TILE).transpose(0, 2, 1, 3)
    return shaped.reshape(D, KV)

def reference(activations, cotangent, next_inputs, weight_tiles, momentum, chosen, counts):
    highest = lax.Precision.HIGHEST
    keep_rows = cosine_rows(KEEP)
    grad_scale = 1.0 / math.sqrt(ROWS_REP)
    act_groups = activations.reshape(REPLICAS, TOK_SHARDS, TOK_DEV, D)
    cot_groups = cotangent.reshape(REPLICAS, TOK_SHARDS, TOK_DEV, KV)
    slot_ids = jnp.arange(SLOTS, dtype=jnp.int32)
    offsets = (jnp.arange(TOK_SHARDS, dtype=jnp.int32) * TILES_DEV)[:, None]

    def one_replica(summed, replica_data):
        act_rep, cot_rep, moment_rep, chosen_rep, counts_rep = replica_data

        def add_shard(total, shard_data):
            product = jnp.dot(shard_data[0].T, shard_data[1], preferred_element_type=jnp.float32) * grad_scale
            rounded = lax.optimization_barrier(to_tiles(product).astype(jnp.bfloat16))
            return (total + rounded.astype(jnp.float32), None)
        gradient, _ = lax.scan(add_shard, jnp.zeros((TILES, TILE * TILE), jnp.float32), (act_rep, cot_rep))
        updated = momentum_decay * moment_rep + gradient
        global_ids = (offsets + chosen_rep).reshape(-1).astype(jnp.int32)
        in_list = (slot_ids[None, :] < counts_rep[:, None]).reshape(-1)
        picked = updated[global_ids].reshape(-1, TILE, TILE)
        quadrant = jnp.einsum('ua,nab,vb->nuv', keep_rows, picked, keep_rows, precision=highest)
        quadrant = lax.optimization_barrier(jnp.where(in_list[:, None, None], quadrant, 0.0).astype(jnp.bfloat16))
        quadrant = quadrant.astype(jnp.float32)
        rebuilt = jnp.einsum('ua,nuv,vb->nab', keep_rows, quadrant, keep_rows, precision=highest)
        residual = updated.at[global_ids].add(-rebuilt.reshape(-1, TILE * TILE))
        summed = summed.at[global_ids].add(quadrant.reshape(-1, KEEP * KEEP))
        return (summed, residual)
    summed, new_momentum = lax.scan(one_replica, jnp.zeros((TILES, KEEP * KEEP), jnp.float32), (act_groups, cot_groups, momentum, chosen, counts))
    update = jnp.einsum('ua,tuv,vb->tab', keep_rows, summed.reshape(TILES, KEEP, KEEP), keep_rows, precision=highest)
    new_tiles = (weight_tiles.astype(jnp.float32) - step_size * update.reshape(TILES, TILE * TILE)).astype(jnp.bfloat16)
    values = jnp.dot(next_inputs, from_tiles(new_tiles), preferred_element_type=jnp.float32).astype(jnp.bfloat16)
    return (values, new_momentum)
```

```python
import functools
import math

import jax
import jax.numpy as jnp
import numpy as np
from jax import lax
from jax.experimental import pallas as pl
from jax.experimental.pallas import tpu as pltpu
from jax.sharding import PartitionSpec as P

TILE = 64
KEEP = 32
CHIP_TILES = 30
CHIP_PAIRS = 15
PAIRS = 8
XS = 4

momentum_decay = 0.9
step_size = 0.01
F32 = jnp.float32
BF16 = jnp.bfloat16


def cosine_table():
    frequency = np.arange(KEEP)[:, None]
    position = np.arange(TILE)[None, :]
    cosines = np.cos(math.pi * (2.0 * position + 1.0) * frequency / (2.0 * TILE))
    factor = np.where(frequency == 0, math.sqrt(1.0 / TILE), math.sqrt(2.0 / TILE))
    return (cosines * factor).astype(np.float32)


def tables(col_tiles):
    low = cosine_table()
    fine = np.zeros((352, 128), np.float32)
    fine[0:32, 0:64] = low
    fine[32:96, 0:32] = low.T
    two = np.kron(np.eye(2, dtype=np.float32), low.T)
    fine[96:224, 0:64] = two
    fine[96:224, 64:128] = two
    fine[224:288, :] = two.T
    rows_low = np.kron(np.eye(4, dtype=np.float32), low.T)
    cols_low = np.kron(np.eye(col_tiles, dtype=np.float32), low)
    return fine, rows_low.astype(jnp.bfloat16), cols_low.astype(jnp.bfloat16)


def fold_sources(z_size, doubles):
    made = [[] for _ in range(doubles)]
    for z in range(z_size):
        for c in range(2):
            first = CHIP_PAIRS * z + 7 * c
            for p in range(PAIRS):
                pair = first + p
                block = p // 2 if first % 2 == 0 else ((p + 1) // 2) % 4
                lo = 64 * (pair % 2)
                hi = lo + 64
                if c == 0 and p == 7:
                    hi -= 32
                if c == 1 and p == 0:
                    lo += 32
                made[pair // 2].append((c, z, block, lo, hi))
    joined = []
    for parts in made:
        blocks = {}
        for c, z, block, lo, hi in parts:
            old = blocks.get((c, z, block), (lo, hi))
            blocks[c, z, block] = (min(old[0], lo), max(old[1], hi))
        joined.append([(k, v) for k, v in blocks.items()])
    return joined


def kernel(
    Y, Z, scale,
    at_ref, cot_ref, xt_ref, w_ref, mom_ref, chosen_ref, counts_ref, fine_ref, rl_ref, cl_ref,
    values_ref, newm_ref,
    a_own, c_own, a_sib, c_sib, xt, xr, low_in, wall, wmat, wfold, mfold, wpair, u0, grad, prod, own,
    send_p, send_m, got_p, got_m, pack, ys, xs, sall, smat, base, nfold,
    load_sem, a_send, a_recv, c_send, c_recv,
    rp_send, rp_recv, rm_send, rm_recv,
    wz_send, wz_recv, wy_send, wy_recv, wx_send, wx_recv, wc_send, wc_recv,
    sz_send, sz_recv, sy_send, sy_recv, sx_send, sx_recv, sc_send, sc_recv,
    ry_send, ry_recv, rx_send, rx_recv, out_sem,
):
    H = Z // 2
    ZS = Z // XS
    UP = PAIRS // Y
    D = at_ref.shape[0]
    RT = D // TILE
    KB = xr.shape[1] // 256
    replica, tok = lax.axis_index("replica"), lax.axis_index("tok")
    y, x = replica // XS, replica % XS
    z, c = tok // 2, tok % 2
    me = (replica, tok)
    sib = (replica, z * 2 + (1 - c))

    def at_z(o):
        return (replica, ((z + o) % Z) * 2 + c)

    def at_y(o):
        return (((y + o) % Y) * XS + x, tok)

    def at_x(o):
        return (y * XS + (x + o) % XS, tok)

    def rc(src, dst, ss, rs, dev):
        return pltpu.make_async_remote_copy(
            src_ref=src, dst_ref=dst, send_sem=ss, recv_sem=rs,
            device_id=dev, device_id_type=pl.DeviceIdType.MESH)

    def dot(a, b):
        return lax.dot_general(a, b, (((1,), (0,)), ((), ())), preferred_element_type=F32)

    def dot_fine(a, b):
        return lax.dot_general(a, b, (((1,), (0,)), ((), ())), preferred_element_type=F32,
                               precision=lax.Precision.HIGHEST)

    loads = [
        pltpu.make_async_copy(cot_ref, c_own, load_sem.at[0]),
        pltpu.make_async_copy(at_ref, a_own, load_sem.at[1]),
        pltpu.make_async_copy(w_ref, wfold.at[pl.ds(1, 15)], load_sem.at[2]),
        pltpu.make_async_copy(mom_ref, mfold.at[pl.ds(1, 15)], load_sem.at[3]),
        pltpu.make_async_copy(xt_ref, xt.at[pl.ds(0, D)], load_sem.at[4]),
    ]

    barrier = pltpu.get_barrier_semaphore()
    pl.semaphore_signal(barrier, inc=1, device_id=sib, device_id_type=pl.DeviceIdType.MESH)
    for o in range(1, Z):
        pl.semaphore_signal(barrier, inc=1, device_id=at_z(o), device_id_type=pl.DeviceIdType.MESH)
    for o in range(1, Y):
        pl.semaphore_signal(barrier, inc=1, device_id=at_y(o), device_id_type=pl.DeviceIdType.MESH)
    for o in range(1, XS):
        pl.semaphore_signal(barrier, inc=1, device_id=at_x(o), device_id_type=pl.DeviceIdType.MESH)
    for load in loads:
        load.start()

    lane = lax.broadcasted_iota(jnp.int32, (32, 128), 1)
    left = lane < 64

    wfold[0] = jnp.zeros((32, 128), BF16)
    wfold[16] = jnp.zeros((32, 128), BF16)
    mfold[0] = jnp.zeros((32, 128), F32)
    mfold[16] = jnp.zeros((32, 128), F32)
    got_p[0, 4:8] = jnp.zeros((4, TILE, 128), BF16)
    got_m[0, 0:4] = jnp.zeros((4, TILE, 128), BF16)
    if KB * 256 > D:
        xt[D:, :] = jnp.zeros((KB * 256 - D, xt.shape[1]), BF16)
        wmat[D:, :] = jnp.zeros((KB * 256 - D, wmat.shape[1]), BF16)
        smat[D // 2:, :] = jnp.zeros((KB * 128 - D // 2, smat.shape[1]), BF16)

    pl.semaphore_wait(barrier, Z + Y + XS - 2)

    def row_start(e, core):
        dest = (z + e) % Z
        return jnp.minimum((CHIP_PAIRS * dest + 7 * core) // 4, RT - 3) * TILE

    def a_copy(e):
        rows = pl.ds(pl.multiple_of(row_start(e, 1 - c), TILE), 3 * TILE)
        return rc(at_ref.at[rows], a_sib.at[e], a_send.at[e], a_recv.at[e], sib)

    c_copy = rc(cot_ref, c_sib, c_send, c_recv, sib)
    c_copy.start()
    a_copy(H).start()

    @pl.loop(1, H)
    def _(s):
        a_copy(H - s).start()
        a_copy(H + s).start()

    a_copy(0).start()

    class Spread:
        def __init__(self, buf, zs_, zr, ys_, yr, xs_, xr_, cs, cr):
            self.buf, self.zs, self.zr, self.ys, self.yr = buf, zs_, zr, ys_, yr
            self.xs, self.xr, self.cs, self.cr = xs_, xr_, cs, cr

        def mine(self):
            return self.buf.at[c, x, pl.ds(UP * y, UP)]

        def z_copy(self, o):
            part = self.mine().at[:, z // XS]
            return rc(part, part, self.zs.at[o - 1], self.zr.at[z // XS], at_z(o))

        def start_z(self):
            @pl.when(z % XS == x)
            def _():
                @pl.loop(1, Z)
                def _(o):
                    self.z_copy(o).start()

        def wait_z(self):
            @pl.loop(0, ZS)
            def _(k):
                @pl.when(z != x + XS * k)
                def _():
                    part = self.mine().at[:, k]
                    rc(part, part, self.zs.at[0], self.zr.at[k], at_z(1)).wait_recv()

        def y_copy(self, o):
            return rc(self.mine(), self.mine(), self.ys.at[o - 1], self.yr.at[o - 1], at_y(o))

        def start_y(self):
            @pl.loop(1, Y)
            def _(o):
                self.y_copy(o).start()

        def wait_y(self):
            @pl.loop(1, Y)
            def _(o):
                part = self.buf.at[c, x, pl.ds(UP * ((y + Y - o) % Y), UP)]
                rc(part, part, self.ys.at[o - 1], self.yr.at[o - 1], at_y(1)).wait_recv()

        def x_copy(self, k):
            if k < 2:
                part = self.buf.at[c, x]
            else:
                near = (x + XS - 1) % XS if k == 2 else (x + 1) % XS
                part = self.buf.at[c, near, pl.ds(0 if k == 2 else 4, 4)]
            return rc(part, part, self.xs.at[k], self.xr.at[k], at_x(1 if k % 2 == 0 else XS - 1))

        def c_copy(self, k):
            part = self.buf.at[c, (x + k) % XS]
            return rc(part, part, self.cs.at[k], self.cr.at[k], sib)

        def start_x(self):
            self.x_copy(0).start()
            self.x_copy(1).start()
            self.c_copy(0).start()

        def forward_x(self):
            from_left = self.buf.at[c, (x + XS - 1) % XS]
            rc(from_left, from_left, self.xs.at[0], self.xr.at[0], at_x(1)).wait_recv()
            self.x_copy(2).start()
            self.c_copy(3).start()
            from_right = self.buf.at[c, (x + 1) % XS]
            rc(from_right, from_right, self.xs.at[1], self.xr.at[1], at_x(1)).wait_recv()
            self.x_copy(3).start()
            self.c_copy(1).start()

        def finish_x(self):
            far = (x + 2) % XS
            for k in (2, 3):
                part = self.buf.at[c, far, pl.ds(0 if k == 2 else 4, 4)]
                rc(part, part, self.xs.at[k], self.xr.at[k], at_x(1)).wait_recv()
            self.c_copy(2).start()

        def wait_core(self):
            for k in range(XS):
                part = self.buf.at[1 - c, (x + k) % XS]
                rc(part, part, self.cs.at[k], self.cr.at[k], sib).wait_recv()

        def wait_sends(self):
            @pl.when(z % XS == x)
            def _():
                @pl.loop(1, Z)
                def _(o):
                    self.z_copy(o).wait_send()

            @pl.loop(1, Y)
            def _(o):
                self.y_copy(o).wait_send()

            for k in range(4):
                self.x_copy(k).wait_send()
            for k in range(XS):
                self.c_copy(k).wait_send()

    wide = Spread(wall, wz_send, wz_recv, wy_send, wy_recv, wx_send, wx_recv, wc_send, wc_recv)
    quads = Spread(sall, sz_send, sz_recv, sy_send, sy_recv, sx_send, sx_recv, sc_send, sc_recv)

    def unfold(fold_ref, p):
        first = fold_ref[1 + 2 * p - c].astype(F32)
        second = fold_ref[2 + 2 * p - c].astype(F32)
        even = jnp.where(left, first, pltpu.roll(second, 64, 1))
        odd = jnp.where(left, pltpu.roll(first, 64, 1), second)
        return even, odd

    loads[2].wait()

    @pl.when(z % XS == x)
    def _():
        for k in range(UP):
            even, odd = unfold(wfold, UP * y + k)
            wpair[pl.ds(0, 32, stride=2), :] = even
            wpair[pl.ds(1, 32, stride=2), :] = odd
            wall[c, x, UP * y + k, z // XS] = wpair[...].astype(BF16)

    wide.start_z()

    loads[0].wait()
    loads[1].wait()
    rc(c_sib, c_sib, c_send, c_recv, sib).wait_recv()

    def partial(e, slot):
        rc(a_sib.at[e], a_sib.at[e], a_send.at[e], a_recv.at[e], sib).wait_recv()
        start = row_start(e, c)
        rows = pl.ds(pl.multiple_of(start, TILE), 3 * TILE)
        total = dot(a_own[rows, :], c_own[...]) + dot(a_sib[e], c_sib[...])
        total = total * scale
        for j in range(4):
            prod[j] = total[:, 128 * j:128 * j + 128]
        first = CHIP_PAIRS * ((z + e) % Z) + 7 * c
        for p in range(PAIRS):
            pair = first + p
            row = pl.multiple_of((pair // 4) * TILE - start, TILE)
            own[slot, p] = prod[pair % 4, pl.ds(row, TILE), :]

    def p_copy(s, h):
        return rc(send_p.at[s, pl.ds(4 * h, 4)], got_p.at[s, pl.ds(4 * h, 4)],
                  rp_send.at[s, h], rp_recv.at[s, h], at_z(1))

    def m_copy(s, h):
        return rc(send_m.at[s, pl.ds(4 * h, 4)], got_m.at[s, pl.ds(4 * h, 4)],
                  rm_send.at[s, h], rm_recv.at[s, h], at_z(Z - 1))

    partial(H, 0)
    send_p[0, 0:4] = own[0, 0:4].astype(BF16)
    p_copy(0, 0).start()
    send_m[0, 4:8] = own[0, 4:8].astype(BF16)
    m_copy(0, 1).start()

    @pl.loop(1, H)
    def _(s):
        partial(H - s, 0)
        partial(H + s, 1)
        for step in range(2):
            hp, hm = step, 1 - step
            if step == 0:
                p_copy(s - 1, hp).wait_recv()
            else:
                @pl.when(s > 1)
                def _():
                    p_copy(s - 1, hp).wait_recv()
            part = own[0, 4 * hp:4 * hp + 4] + got_p[s - 1, 4 * hp:4 * hp + 4].astype(F32)
            send_p[s, 4 * hp:4 * hp + 4] = part.astype(BF16)
            p_copy(s, hp).start()
            if step == 0:
                m_copy(s - 1, hm).wait_recv()
            else:
                @pl.when(s > 1)
                def _():
                    m_copy(s - 1, hm).wait_recv()
            part = own[1, 4 * hm:4 * hm + 4] + got_m[s - 1, 4 * hm:4 * hm + 4].astype(F32)
            send_m[s, 4 * hm:4 * hm + 4] = part.astype(BF16)
            m_copy(s, hm).start()

        @pl.when(s == 1)
        def _():
            wide.wait_z()
            wide.start_y()

        @pl.when(s == min(3, H - 1))
        def _():
            wide.wait_y()
            wide.start_x()

    partial(0, 0)

    loads[3].wait()
    for p in range(PAIRS):
        even, odd = unfold(mfold, p)
        u0[p, pl.ds(0, 32, stride=2), :] = even * momentum_decay
        u0[p, pl.ds(1, 32, stride=2), :] = odd * momentum_decay
    for p in range(PAIRS):
        own[0, p] = own[0, p] + u0[p]

    shape = (PAIRS * KEEP, 128)
    number = 2 * (lax.broadcasted_iota(jnp.int32, shape, 0) // KEEP) - c
    number = number + (lax.broadcasted_iota(jnp.int32, shape, 1) // KEEP) % 2
    keep = jnp.zeros(shape, F32)
    for s in range(8):
        listed = jnp.where(s < counts_ref[0], chosen_ref[s], -5)
        keep = jnp.where(number == listed, 1.0, keep)

    for h in range(2):
        p_copy(H - 1, h).wait_recv()
        m_copy(H - 1, h).wait_recv()
    for p in range(PAIRS):
        grad[p] = own[0, p] + (got_p[H - 1, p].astype(F32) + got_m[H - 1, p].astype(F32))

    low = fine_ref[0:32, 0:64]
    side = dot_fine(low, jnp.concatenate([grad[p] for p in range(PAIRS)], axis=1))
    side = jnp.concatenate([side[:, 128 * p:128 * p + 128] for p in range(PAIRS)], axis=0)
    quad = dot_fine(side, fine_ref[96:224, :])
    quad = jnp.where(keep > 0.5, quad, 0.0).astype(BF16).astype(F32)
    odd_first = ((z + c) % 2) == 1
    for d in range(4):
        blocks = [quad[32 * p:32 * p + 32] for p in range(PAIRS)]
        plain = jnp.where(left, blocks[2 * d], blocks[2 * d + 1])
        turned = jnp.where(left, blocks[(2 * d + 7) % 8], blocks[2 * d])
        block = jnp.where(odd_first, turned, plain).astype(BF16)
        pack[2 * d] = block[0:16]
        pack[2 * d + 1] = block[16:32]

    def ry_copy(o):
        return rc(pack.at[pl.ds(UP * ((y + o) % Y), UP)], ys.at[o - 1],
                  ry_send.at[o - 1], ry_recv.at[o - 1], at_y(o))

    @pl.loop(1, Y)
    def _(o):
        ry_copy(o).start()

    wide.forward_x()

    @pl.loop(1, Y)
    def _(o):
        ry_copy(o).wait_recv()

    total = pack[pl.ds(UP * y, UP)].astype(F32)
    for o in range(1, Y):
        total = total + ys[o - 1].astype(F32)
    xs[0] = total

    def rx_copy(o):
        return rc(xs.at[0], xs.at[o], rx_send.at[o - 1], rx_recv.at[o - 1], at_x(o))

    for o in range(1, XS):
        rx_copy(o).start()

    quad_side = dot_fine(quad[:, 0:64], fine_ref[224:288, :])
    quad_side = jnp.concatenate([quad_side[32 * p:32 * p + 32] for p in range(PAIRS)], axis=1)
    shift = dot_fine(fine_ref[32:96, 0:32], quad_side)
    for p in range(PAIRS):
        grad[p] = grad[p] - shift[:, 128 * p:128 * p + 128]

    for o in range(1, XS):
        rx_copy(o).wait_recv()
    total = (xs[0] + xs[2]) + (xs[1] + xs[3])

    @pl.when(z % XS == x)
    def _():
        for k in range(UP):
            sall[c, x, UP * y + k, z // XS] = total[k].astype(BF16)

    quads.start_z()

    for p in range(PAIRS):
        even = grad[p, pl.ds(0, 32, stride=2), :]
        odd = grad[p, pl.ds(1, 32, stride=2), :]
        nfold[1 + 2 * p - c] = jnp.where(left, even, pltpu.roll(odd, 64, 1))
        nfold[2 + 2 * p - c] = jnp.where(left, pltpu.roll(even, 64, 1), odd)
    out_copy = pltpu.make_async_copy(nfold.at[pl.ds(1, 15)], newm_ref, out_sem)
    out_copy.start()

    quads.wait_z()
    quads.start_y()
    loads[4].wait()
    wide.finish_x()

    @pl.loop(0, KB)
    def _(k):
        rows = pl.ds(pl.multiple_of(256 * k, 256), 256)
        xr[:, rows] = xt[rows, :].T

    quads.wait_y()
    quads.start_x()

    @pl.loop(0, KB)
    def _(k):
        rows = pl.ds(pl.multiple_of(256 * k, 256), 256)
        low_in[:, pl.ds(pl.multiple_of(128 * k, 128), 128)] = dot(xr[:, rows], rl_ref[...]).astype(BF16)

    wide.wait_core()
    left64 = lax.broadcasted_iota(jnp.int32, (TILE, 128), 1) < 64
    for zz in range(Z):
        for p in range(CHIP_PAIRS):
            pair = CHIP_PAIRS * zz + p
            core, slot = (0, p) if p < 8 else (1, p - 7)
            block = wall[core, zz % XS, slot, zz // XS]
            if p == 7:
                block = jnp.where(left64, block, wall[1, zz % XS, 0, zz // XS])
            wmat[TILE * (pair // 4):TILE * (pair // 4) + TILE,
                 128 * (pair % 4):128 * (pair % 4) + 128] = block

    quads.forward_x()
    base[...] = jnp.zeros(base.shape, F32)

    @pl.loop(0, KB)
    def _(k):
        rows = pl.ds(pl.multiple_of(256 * k, 256), 256)
        base[...] += dot(xr[:, rows], wmat[rows, :])

    quads.finish_x()
    quads.wait_core()

    lane16 = lax.broadcasted_iota(jnp.int32, (16, 128), 1)
    for n, parts in enumerate(fold_sources(Z, D * 2 // 64)):
        for half in range(2):
            block = None
            for (core, zz, d), (lo, hi) in parts:
                part = sall[core, zz % XS, 2 * d + half, zz // XS]
                if block is None:
                    block = part
                else:
                    block = jnp.where((lane16 >= lo) & (lane16 < hi), part, block)
            row = 32 * (n // 2) + 16 * half
            smat[row:row + 16, 128 * (n % 2):128 * (n % 2) + 128] = block

    late = dot(low_in[...], smat[...]) * step_size
    values_ref[...] = (base[...] - dot(late.astype(BF16), cl_ref[...])).astype(BF16)

    out_copy.wait()
    c_copy.wait_send()

    @pl.loop(0, Z)
    def _(e):
        a_copy(e).wait_send()

    p_copy(0, 0).wait_send()
    m_copy(0, 1).wait_send()

    @pl.loop(1, H)
    def _(s):
        for h in range(2):
            p_copy(s, h).wait_send()
            m_copy(s, h).wait_send()

    @pl.loop(1, Y)
    def _(o):
        ry_copy(o).wait_send()

    for o in range(1, XS):
        rx_copy(o).wait_send()
    wide.wait_sends()
    quads.wait_sends()


def local(Y, Z, activations, cotangent, next_inputs, weight_tiles, momentum, chosen, counts):
    tokens, depth = activations.shape
    width = cotangent.shape[1]
    scale = 1.0 / math.sqrt(tokens * 2 * Z)
    H, ZS, UP = Z // 2, Z // XS, PAIRS // Y
    KB = -(-depth // 256)
    fine, rows_low, cols_low = tables(width // TILE)
    hbm = pl.BlockSpec(memory_space=pl.ANY)
    vmem = pl.BlockSpec(memory_space=pltpu.VMEM)
    smem = pl.BlockSpec(memory_space=pltpu.SMEM)
    dma = pltpu.SemaphoreType.DMA
    spread_sems = [dma((Z - 1,)), dma((ZS,)), dma((Y,)), dma((Y,)), dma((4,)), dma((4,)), dma((4,)), dma((4,))]
    pairs = (PAIRS, TILE, 128)
    scratch = [
        pltpu.VMEM((depth, tokens), BF16),
        pltpu.VMEM((tokens, width), BF16),
        pltpu.VMEM((Z, 3 * TILE, tokens), BF16),
        pltpu.VMEM((tokens, width), BF16),
        pltpu.VMEM((KB * 256, tokens), BF16),
        pltpu.VMEM((tokens, KB * 256), BF16),
        pltpu.VMEM((tokens, KB * 128), BF16),
        pltpu.VMEM((2, XS, PAIRS, ZS, TILE, 128), BF16),
        pltpu.VMEM((KB * 256, width), BF16),
        pltpu.VMEM((17, 32, 128), BF16),
        pltpu.VMEM((17, 32, 128), F32),
        pltpu.VMEM((TILE, 128), F32),
        pltpu.VMEM(pairs, F32),
        pltpu.VMEM(pairs, F32),
        pltpu.VMEM((4, 3 * TILE, 128), F32),
        pltpu.VMEM((2,) + pairs, F32),
        pltpu.VMEM((H,) + pairs, BF16),
        pltpu.VMEM((H,) + pairs, BF16),
        pltpu.VMEM((H,) + pairs, BF16),
        pltpu.VMEM((H,) + pairs, BF16),
        pltpu.VMEM((8, 16, 128), BF16),
        pltpu.VMEM((Y, UP, 16, 128), BF16),
        pltpu.VMEM((XS, UP, 16, 128), F32),
        pltpu.VMEM((2, XS, PAIRS, ZS, 16, 128), BF16),
        pltpu.VMEM((KB * 128, width // 2), BF16),
        pltpu.VMEM((tokens, width), F32),
        pltpu.VMEM((17, 32, 128), F32),
        dma((5,)), dma((Z,)), dma((Z,)), dma(()), dma(()),
        dma((H, 2)), dma((H, 2)), dma((H, 2)), dma((H, 2)),
        *spread_sems, *spread_sems,
        dma((Y,)), dma((Y,)), dma((XS,)), dma((XS,)), dma(()),
    ]
    values, new_momentum = pl.pallas_call(
        functools.partial(kernel, Y, Z, scale),
        out_shape=(
            jax.ShapeDtypeStruct((tokens, width), BF16),
            jax.ShapeDtypeStruct((15, 32, 128), F32),
        ),
        in_specs=[hbm, hbm, hbm, hbm, hbm, smem, smem, vmem, vmem, vmem],
        out_specs=(vmem, hbm),
        scratch_shapes=scratch,
        compiler_params=pltpu.CompilerParams(
            collective_id=0, has_side_effects=True, vmem_limit_bytes=48 * 1024 * 1024),
        cost_estimate=pl.CostEstimate(
            flops=4 * tokens * depth * width, bytes_accessed=8 * tokens * depth, transcendentals=0),
    )(
        activations.T, cotangent, next_inputs.T, weight_tiles.reshape(15, 32, 128),
        momentum.reshape(15, 32, 128), chosen.reshape(8), counts.reshape(1),
        jnp.asarray(fine), jnp.asarray(rows_low), jnp.asarray(cols_low),
    )
    return values, new_momentum.reshape(1, 15, TILE * TILE)


def solution(mesh):
    Y, Z = mesh.shape["replica"] // XS, mesh.shape["tok"] // 2
    return jax.shard_map(
        functools.partial(local, Y, Z),
        mesh=mesh,
        in_specs=(
            P(("replica", "tok"), None),
            P(("replica", "tok"), None),
            P(("replica", "tok"), None),
            P("tok", None),
            P("replica", "tok", None),
            P("replica", "tok", None),
            P("replica", "tok"),
        ),
        out_specs=(P(("replica", "tok"), None), P("replica", "tok", None)),
        check_vma=False,
    )
```

```python
import functools
import math

import jax
import jax.numpy as jnp
import numpy as np
from jax import lax
from jax.experimental import pallas as pl
from jax.experimental.pallas import tpu as pltpu
from jax.sharding import PartitionSpec as P

TILE = 64
KEEP = 32
CHIP_TILES = 30
CHIP_PAIRS = 15
PAIRS = 8
XS = 4

momentum_decay = 0.9
step_size = 0.01
F32 = jnp.float32
BF16 = jnp.bfloat16


def cosine_table():
    frequency = np.arange(KEEP)[:, None]
    position = np.arange(TILE)[None, :]
    cosines = np.cos(math.pi * (2.0 * position + 1.0) * frequency / (2.0 * TILE))
    factor = np.where(frequency == 0, math.sqrt(1.0 / TILE), math.sqrt(2.0 / TILE))
    return (cosines * factor).astype(np.float32)


def split(values):
    high = values.astype(jnp.bfloat16)
    return high, (values - high.astype(jnp.float32)).astype(jnp.bfloat16)


def tables(col_tiles):
    low = cosine_table()
    high_part, low_part = (np.asarray(v, np.float32) for v in split(low))
    two = np.kron(np.eye(2, dtype=np.float32), low.T)
    twice = np.concatenate([two, two], axis=1)
    back = np.concatenate([two.T, np.zeros((64, 128), np.float32)], axis=0)
    fine = np.zeros((768, 128), np.float32)
    fine[0:32, 0:64] = fine[0:32, 64:128] = high_part
    fine[32:64, 0:64] = fine[32:64, 64:128] = low_part
    fine[64:128, 0:32] = fine[64:128, 32:64] = high_part.T
    fine[64:128, 64:96] = low_part.T
    fine[128:256], fine[384:512] = (np.asarray(v, np.float32) for v in split(twice))
    fine[256:384] = fine[128:256]
    fine[512:640], fine[640:768] = (np.asarray(v, np.float32) for v in split(back))
    rows_low = np.kron(np.eye(4, dtype=np.float32), low.T)
    cols_low = np.kron(np.eye(col_tiles, dtype=np.float32), low)
    return fine.astype(jnp.bfloat16), rows_low.astype(jnp.bfloat16), cols_low.astype(jnp.bfloat16)


def fold_sources(z_size, doubles):
    made = [[] for _ in range(doubles)]
    for z in range(z_size):
        for c in range(2):
            first = CHIP_PAIRS * z + 7 * c
            for p in range(PAIRS):
                pair = first + p
                block = p // 2 if first % 2 == 0 else ((p + 1) // 2) % 4
                lo = 64 * (pair % 2)
                hi = lo + 64
                if c == 0 and p == 7:
                    hi -= 32
                if c == 1 and p == 0:
                    lo += 32
                made[pair // 2].append((c, z, block, lo, hi))
    joined = []
    for parts in made:
        blocks = {}
        for c, z, block, lo, hi in parts:
            old = blocks.get((c, z, block), (lo, hi))
            blocks[c, z, block] = (min(old[0], lo), max(old[1], hi))
        joined.append([(k, v) for k, v in blocks.items()])
    return joined


def kernel(
    Y, Z, scale,
    at_ref, cot_ref, xt_ref, w_ref, mom_ref, chosen_in, counts_in, fine_in, rl_in, cl_in,
    values_ref, newm_ref,
    a_own, c_own, a_sib, c_sib, xt, xr, low_in, wall, wmat, wfull, wfold, mfold, wpair, u0, grad, prod, own,
    send_p, send_m, got_p, got_m, pack, ys, xs, sall, smat, base, nfold,
    fine_ref, rl_ref, cl_ref, chosen_ref, counts_ref,
    load_sem, a_send, a_recv, c_send, c_recv,
    rp_send, rp_recv, rm_send, rm_recv,
    wz_send, wz_recv, wy_send, wy_recv, wx_send, wx_recv, wc_send, wc_recv,
    sz_send, sz_recv, sy_send, sy_recv, sx_send, sx_recv, sc_send, sc_recv,
    ry_send, ry_recv, rx_send, rx_recv, out_sem,
):
    H = Z // 2
    ZS = Z // XS
    UP = PAIRS // Y
    D = at_ref.shape[0]
    RT = D // TILE
    KB = xr.shape[1] // 256
    replica, tok = lax.axis_index("replica"), lax.axis_index("tok")
    y, x = replica // XS, replica % XS
    z, c = tok // 2, tok % 2
    me = (replica, tok)
    sib = (replica, z * 2 + (1 - c))

    def at_z(o):
        return (replica, ((z + o) % Z) * 2 + c)

    def at_y(o):
        return (((y + o) % Y) * XS + x, tok)

    def at_x(o):
        return (y * XS + (x + o) % XS, tok)

    def rc(src, dst, ss, rs, dev):
        return pltpu.make_async_remote_copy(
            src_ref=src, dst_ref=dst, send_sem=ss, recv_sem=rs,
            device_id=dev, device_id_type=pl.DeviceIdType.MESH)

    def dot(a, b):
        return lax.dot_general(a, b, (((1,), (0,)), ((), ())), preferred_element_type=F32)

    loads = [
        pltpu.make_async_copy(cot_ref, c_own, load_sem.at[0]),
        pltpu.make_async_copy(at_ref, a_own, load_sem.at[1]),
        pltpu.make_async_copy(w_ref, wfull, load_sem.at[2]),
        pltpu.make_async_copy(mom_ref, mfold.at[pl.ds(1, 15)], load_sem.at[3]),
        pltpu.make_async_copy(xt_ref, xt.at[pl.ds(0, D)], load_sem.at[4]),
        pltpu.make_async_copy(fine_in, fine_ref, load_sem.at[5]),
        pltpu.make_async_copy(rl_in, rl_ref, load_sem.at[6]),
        pltpu.make_async_copy(cl_in, cl_ref, load_sem.at[7]),
        pltpu.make_async_copy(chosen_in, chosen_ref, load_sem.at[8]),
        pltpu.make_async_copy(counts_in, counts_ref, load_sem.at[9]),
    ]

    barrier = pltpu.get_barrier_semaphore()
    pl.semaphore_signal(barrier, inc=1, device_id=sib, device_id_type=pl.DeviceIdType.MESH)
    for o in range(1, Z):
        pl.semaphore_signal(barrier, inc=1, device_id=at_z(o), device_id_type=pl.DeviceIdType.MESH)
    for o in range(1, Y):
        pl.semaphore_signal(barrier, inc=1, device_id=at_y(o), device_id_type=pl.DeviceIdType.MESH)
    for o in range(1, XS):
        pl.semaphore_signal(barrier, inc=1, device_id=at_x(o), device_id_type=pl.DeviceIdType.MESH)
    for load in loads:
        load.start()

    lane = lax.broadcasted_iota(jnp.int32, (32, 128), 1)
    left = lane < 64

    mfold[0] = jnp.zeros((32, 128), F32)
    mfold[16] = jnp.zeros((32, 128), F32)
    got_p[0, 4:8] = jnp.zeros((4, TILE, 128), BF16)
    got_m[0, 0:4] = jnp.zeros((4, TILE, 128), BF16)
    if KB * 256 > D:
        xt[D:, :] = jnp.zeros((KB * 256 - D, xt.shape[1]), BF16)
        wmat[D:, :] = jnp.zeros((KB * 256 - D, wmat.shape[1]), BF16)
        smat[D // 2:, :] = jnp.zeros((KB * 128 - D // 2, smat.shape[1]), BF16)

    pl.semaphore_wait(barrier, Z + Y + XS - 2)

    def row_start(e, core):
        dest = (z + e) % Z
        return jnp.minimum((CHIP_PAIRS * dest + 7 * core) // 4, RT - 3) * TILE

    def a_copy(e):
        rows = pl.ds(pl.multiple_of(row_start(e, 1 - c), TILE), 3 * TILE)
        return rc(at_ref.at[rows], a_sib.at[e], a_send.at[e], a_recv.at[e], sib)

    c_copy = rc(cot_ref, c_sib, c_send, c_recv, sib)
    c_copy.start()
    a_copy(H).start()

    @pl.loop(1, H)
    def _(s):
        a_copy(H - s).start()
        a_copy(H + s).start()

    a_copy(0).start()

    class Spread:
        def __init__(self, buf, zs_, zr, ys_, yr, xs_, xr_, cs, cr):
            self.buf, self.zs, self.zr, self.ys, self.yr = buf, zs_, zr, ys_, yr
            self.xs, self.xr, self.cs, self.cr = xs_, xr_, cs, cr

        def mine(self):
            return self.buf.at[c, x, pl.ds(UP * y, UP)]

        def z_copy(self, o):
            part = self.mine().at[:, z // XS]
            return rc(part, part, self.zs.at[o - 1], self.zr.at[z // XS], at_z(o))

        def start_z(self):
            @pl.when(z % XS == x)
            def _():
                @pl.loop(1, Z)
                def _(o):
                    self.z_copy(o).start()

        def wait_z(self):
            @pl.loop(0, ZS)
            def _(k):
                @pl.when(z != x + XS * k)
                def _():
                    part = self.mine().at[:, k]
                    rc(part, part, self.zs.at[0], self.zr.at[k], at_z(1)).wait_recv()

        def y_copy(self, o):
            return rc(self.mine(), self.mine(), self.ys.at[o - 1], self.yr.at[o - 1], at_y(o))

        def start_y(self):
            @pl.loop(1, Y)
            def _(o):
                self.y_copy(o).start()

        def wait_y(self):
            @pl.loop(1, Y)
            def _(o):
                part = self.buf.at[c, x, pl.ds(UP * ((y + Y - o) % Y), UP)]
                rc(part, part, self.ys.at[o - 1], self.yr.at[o - 1], at_y(1)).wait_recv()

        def x_copy(self, k):
            if k < 2:
                part = self.buf.at[c, x]
            else:
                near = (x + XS - 1) % XS if k == 2 else (x + 1) % XS
                part = self.buf.at[c, near, pl.ds(0 if k == 2 else 4, 4)]
            return rc(part, part, self.xs.at[k], self.xr.at[k], at_x(1 if k % 2 == 0 else XS - 1))

        def c_copy(self, k):
            part = self.buf.at[c, (x + k) % XS]
            return rc(part, part, self.cs.at[k], self.cr.at[k], sib)

        def start_x(self):
            self.x_copy(0).start()
            self.x_copy(1).start()
            self.c_copy(0).start()

        def forward_x(self):
            from_left = self.buf.at[c, (x + XS - 1) % XS]
            rc(from_left, from_left, self.xs.at[0], self.xr.at[0], at_x(1)).wait_recv()
            self.x_copy(2).start()
            self.c_copy(3).start()
            from_right = self.buf.at[c, (x + 1) % XS]
            rc(from_right, from_right, self.xs.at[1], self.xr.at[1], at_x(1)).wait_recv()
            self.x_copy(3).start()
            self.c_copy(1).start()

        def finish_x(self):
            far = (x + 2) % XS
            for k in (2, 3):
                part = self.buf.at[c, far, pl.ds(0 if k == 2 else 4, 4)]
                rc(part, part, self.xs.at[k], self.xr.at[k], at_x(1)).wait_recv()
            self.c_copy(2).start()

        def wait_core(self):
            for k in range(XS):
                part = self.buf.at[1 - c, (x + k) % XS]
                rc(part, part, self.cs.at[k], self.cr.at[k], sib).wait_recv()

        def wait_sends(self):
            @pl.when(z % XS == x)
            def _():
                @pl.loop(1, Z)
                def _(o):
                    self.z_copy(o).wait_send()

            @pl.loop(1, Y)
            def _(o):
                self.y_copy(o).wait_send()

            for k in range(4):
                self.x_copy(k).wait_send()
            for k in range(XS):
                self.c_copy(k).wait_send()

    wide = Spread(wall, wz_send, wz_recv, wy_send, wy_recv, wx_send, wx_recv, wc_send, wc_recv)
    quads = Spread(sall, sz_send, sz_recv, sy_send, sy_recv, sx_send, sx_recv, sc_send, sc_recv)

    def unfold(first, second):
        even = jnp.where(left, first, pltpu.roll(second, 64, 1))
        odd = jnp.where(left, pltpu.roll(first, 64, 1), second)
        return even, odd

    loads[2].wait()

    @pl.when(z % XS == x)
    def _():
        for k in range(UP):
            number = 2 * (UP * y + k) - c
            rows = lax.broadcasted_iota(jnp.int32, (15, 4096), 0)
            for tile in range(2):
                only = jnp.where(rows == number + tile, wfull[...].astype(F32), 0.0)
                only = jnp.sum(only, axis=0, keepdims=True)
                for r in range(32):
                    wfold[tile, r:r + 1, :] = only[:, 128 * r:128 * r + 128]
            even, odd = unfold(wfold[0], wfold[1])
            wpair[pl.ds(0, 32, stride=2), :] = even
            wpair[pl.ds(1, 32, stride=2), :] = odd
            wall[c, x, UP * y + k, z // XS] = wpair[...].astype(BF16)

    wide.start_z()

    loads[0].wait()
    loads[1].wait()
    rc(c_sib, c_sib, c_send, c_recv, sib).wait_recv()

    def partial(e, slot):
        rc(a_sib.at[e], a_sib.at[e], a_send.at[e], a_recv.at[e], sib).wait_recv()
        start = row_start(e, c)
        rows = pl.ds(pl.multiple_of(start, TILE), 3 * TILE)
        total = dot(a_own[rows, :], c_own[...]) + dot(a_sib[e], c_sib[...])
        total = total * scale
        for j in range(4):
            prod[j] = total[:, 128 * j:128 * j + 128]
        first = CHIP_PAIRS * ((z + e) % Z) + 7 * c
        for p in range(PAIRS):
            pair = first + p
            row = pl.multiple_of((pair // 4) * TILE - start, TILE)
            own[slot, p] = prod[pair % 4, pl.ds(row, TILE), :]

    def p_copy(s, h):
        return rc(send_p.at[s, pl.ds(4 * h, 4)], got_p.at[s, pl.ds(4 * h, 4)],
                  rp_send.at[s, h], rp_recv.at[s, h], at_z(1))

    def m_copy(s, h):
        return rc(send_m.at[s, pl.ds(4 * h, 4)], got_m.at[s, pl.ds(4 * h, 4)],
                  rm_send.at[s, h], rm_recv.at[s, h], at_z(Z - 1))

    partial(H, 0)
    send_p[0, 0:4] = own[0, 0:4].astype(BF16)
    p_copy(0, 0).start()
    send_m[0, 4:8] = own[0, 4:8].astype(BF16)
    m_copy(0, 1).start()
    wide.wait_z()
    wide.start_y()
    partial(H - 1, 2)
    partial(H + 1, 3)

    @pl.loop(1, H)
    def _(s):
        now, later = 2 * (s % 2), 2 * ((s + 1) % 2)

        def pass_on(copy, got, send, slot, h, first):
            @pl.when(jnp.logical_or(s > 1, first))
            def _():
                copy(s - 1, h).wait_recv()

            part = own[slot, 4 * h:4 * h + 4] + got[s - 1, 4 * h:4 * h + 4].astype(F32)
            send[s, 4 * h:4 * h + 4] = part.astype(BF16)
            copy(s, h).start()

        pass_on(p_copy, got_p, send_p, now, 0, True)
        pass_on(m_copy, got_m, send_m, now + 1, 1, True)
        partial(H - 1 - s, later)
        pass_on(p_copy, got_p, send_p, now, 1, False)
        pass_on(m_copy, got_m, send_m, now + 1, 0, False)

        @pl.when(s < H - 1)
        def _():
            partial(H + 1 + s, later + 1)

        @pl.when(s == min(4, H - 1))
        def _():
            wide.wait_y()
            wide.start_x()

    last = 2 * (H % 2)

    loads[3].wait()
    loads[5].wait()
    loads[8].wait()
    loads[9].wait()
    for p in range(PAIRS):
        even, odd = unfold(mfold[1 + 2 * p - c], mfold[2 + 2 * p - c])
        u0[p, pl.ds(0, 32, stride=2), :] = even * momentum_decay
        u0[p, pl.ds(1, 32, stride=2), :] = odd * momentum_decay
    for p in range(PAIRS):
        u0[p] = own[last, p] + u0[p]
    high, rest = split(jnp.concatenate([u0[p] for p in range(PAIRS)], axis=1))
    side_own = dot(fine_ref[0:64, 0:64], high)
    side_own = side_own[0:32] + side_own[32:64] + dot(fine_ref[0:32, 0:64], rest)

    shape = (PAIRS * KEEP, 128)
    number = 2 * (lax.broadcasted_iota(jnp.int32, shape, 0) // KEEP) - c
    number = number + (lax.broadcasted_iota(jnp.int32, shape, 1) // KEEP) % 2
    keep = jnp.zeros(shape, F32)
    for s in range(8):
        listed = jnp.where(s < counts_ref[0, 0], chosen_ref[0, s], -5)
        keep = jnp.where(number == listed, 1.0, keep)

    for h in range(2):
        p_copy(H - 1, h).wait_recv()
        m_copy(H - 1, h).wait_recv()
    arrived = jnp.concatenate(
        [jnp.concatenate([got[H - 1, p] for p in range(PAIRS)], axis=1) for got in (got_p, got_m)], axis=0)
    side = dot(fine_ref[0:64, :], arrived)
    side = side_own + (side[0:32] + side[32:64])
    side = jnp.concatenate([side[:, 128 * p:128 * p + 128] for p in range(PAIRS)], axis=0)
    high, rest = split(side)
    quad = dot(jnp.concatenate([high, rest, high], axis=1), fine_ref[128:512, :])
    quad = jnp.where(keep > 0.5, quad, 0.0).astype(BF16).astype(F32)
    odd_first = ((z + c) % 2) == 1
    for d in range(4):
        blocks = [quad[32 * p:32 * p + 32] for p in range(PAIRS)]
        plain = jnp.where(left, blocks[2 * d], blocks[2 * d + 1])
        turned = jnp.where(left, blocks[(2 * d + 7) % 8], blocks[2 * d])
        block = jnp.where(odd_first, turned, plain).astype(BF16)
        pack[2 * d] = block[0:16]
        pack[2 * d + 1] = block[16:32]

    def ry_copy(o):
        return rc(pack.at[pl.ds(UP * ((y + o) % Y), UP)], ys.at[o - 1],
                  ry_send.at[o - 1], ry_recv.at[o - 1], at_y(o))

    @pl.loop(1, Y)
    def _(o):
        ry_copy(o).start()

    wide.forward_x()

    @pl.loop(1, Y)
    def _(o):
        ry_copy(o).wait_recv()

    total = pack[pl.ds(UP * y, UP)].astype(F32)
    for o in range(1, Y):
        total = total + ys[o - 1].astype(F32)
    xs[0] = total

    def rx_copy(o):
        return rc(xs.at[0], xs.at[o], rx_send.at[o - 1], rx_recv.at[o - 1], at_x(o))

    for o in range(1, XS):
        rx_copy(o).start()

    exact = quad.astype(BF16)
    quad_side = dot(jnp.concatenate([exact, exact], axis=1), fine_ref[512:768, :])
    quad_side = jnp.concatenate([quad_side[32 * p:32 * p + 32] for p in range(PAIRS)], axis=1)
    high, rest = split(quad_side)
    shift = dot(fine_ref[64:128, 0:96], jnp.concatenate([high, rest, high], axis=0))
    for p in range(PAIRS):
        got = got_p[H - 1, p].astype(F32) + got_m[H - 1, p].astype(F32)
        grad[p] = (u0[p] + got) - shift[:, 128 * p:128 * p + 128]

    for o in range(1, XS):
        rx_copy(o).wait_recv()
    total = (xs[0] + xs[2]) + (xs[1] + xs[3])

    @pl.when(z % XS == x)
    def _():
        for k in range(UP):
            sall[c, x, UP * y + k, z // XS] = total[k].astype(BF16)

    quads.start_z()

    for p in range(PAIRS):
        even = grad[p, pl.ds(0, 32, stride=2), :]
        odd = grad[p, pl.ds(1, 32, stride=2), :]
        nfold[1 + 2 * p - c] = jnp.where(left, even, pltpu.roll(odd, 64, 1))
        nfold[2 + 2 * p - c] = jnp.where(left, pltpu.roll(even, 64, 1), odd)
    out_copy = pltpu.make_async_copy(nfold.at[pl.ds(1, 15)], newm_ref, out_sem)
    out_copy.start()

    quads.wait_z()
    quads.start_y()
    loads[4].wait()
    loads[6].wait()
    loads[7].wait()
    wide.finish_x()

    @pl.loop(0, KB)
    def _(k):
        rows = pl.ds(pl.multiple_of(256 * k, 256), 256)
        xr[:, rows] = xt[rows, :].T

    quads.wait_y()
    quads.start_x()

    @pl.loop(0, KB)
    def _(k):
        rows = pl.ds(pl.multiple_of(256 * k, 256), 256)
        low_in[:, pl.ds(pl.multiple_of(128 * k, 128), 128)] = dot(xr[:, rows], rl_ref[...]).astype(BF16)

    wide.wait_core()
    left64 = lax.broadcasted_iota(jnp.int32, (TILE, 128), 1) < 64
    for zz in range(Z):
        for p in range(CHIP_PAIRS):
            pair = CHIP_PAIRS * zz + p
            core, slot = (0, p) if p < 8 else (1, p - 7)
            block = wall[core, zz % XS, slot, zz // XS]
            if p == 7:
                block = jnp.where(left64, block, wall[1, zz % XS, 0, zz // XS])
            wmat[TILE * (pair // 4):TILE * (pair // 4) + TILE,
                 128 * (pair % 4):128 * (pair % 4) + 128] = block

    quads.forward_x()
    base[...] = jnp.zeros(base.shape, F32)

    @pl.loop(0, KB)
    def _(k):
        rows = pl.ds(pl.multiple_of(256 * k, 256), 256)
        base[...] += dot(xr[:, rows], wmat[rows, :])

    quads.finish_x()
    quads.wait_core()

    lane16 = lax.broadcasted_iota(jnp.int32, (16, 128), 1)
    for n, parts in enumerate(fold_sources(Z, D * 2 // 64)):
        for half in range(2):
            block = None
            for (core, zz, d), (lo, hi) in parts:
                part = sall[core, zz % XS, 2 * d + half, zz // XS]
                if block is None:
                    block = part
                else:
                    block = jnp.where((lane16 >= lo) & (lane16 < hi), part, block)
            row = 32 * (n // 2) + 16 * half
            smat[row:row + 16, 128 * (n % 2):128 * (n % 2) + 128] = block

    late = dot(low_in[...], smat[...]) * step_size
    values_ref[...] = (base[...] - dot(late.astype(BF16), cl_ref[...])).astype(BF16)

    out_copy.wait()
    c_copy.wait_send()

    @pl.loop(0, Z)
    def _(e):
        a_copy(e).wait_send()

    p_copy(0, 0).wait_send()
    m_copy(0, 1).wait_send()

    @pl.loop(1, H)
    def _(s):
        for h in range(2):
            p_copy(s, h).wait_send()
            m_copy(s, h).wait_send()

    @pl.loop(1, Y)
    def _(o):
        ry_copy(o).wait_send()

    for o in range(1, XS):
        rx_copy(o).wait_send()
    wide.wait_sends()
    quads.wait_sends()


def local(Y, Z, activations, cotangent, next_inputs, weight_tiles, momentum, chosen, counts):
    tokens, depth = activations.shape
    width = cotangent.shape[1]
    scale = 1.0 / math.sqrt(tokens * 2 * Z)
    H, ZS, UP = Z // 2, Z // XS, PAIRS // Y
    KB = -(-depth // 256)
    fine, rows_low, cols_low = tables(width // TILE)
    hbm = pl.BlockSpec(memory_space=pl.ANY)
    vmem = pl.BlockSpec(memory_space=pltpu.VMEM)
    dma = pltpu.SemaphoreType.DMA
    spread_sems = [dma((Z - 1,)), dma((ZS,)), dma((Y,)), dma((Y,)), dma((4,)), dma((4,)), dma((4,)), dma((4,))]
    pairs = (PAIRS, TILE, 128)
    scratch = [
        pltpu.VMEM((depth, tokens), BF16),
        pltpu.VMEM((tokens, width), BF16),
        pltpu.VMEM((Z, 3 * TILE, tokens), BF16),
        pltpu.VMEM((tokens, width), BF16),
        pltpu.VMEM((KB * 256, tokens), BF16),
        pltpu.VMEM((tokens, KB * 256), BF16),
        pltpu.VMEM((tokens, KB * 128), BF16),
        pltpu.VMEM((2, XS, PAIRS, ZS, TILE, 128), BF16),
        pltpu.VMEM((KB * 256, width), BF16),
        pltpu.VMEM((15, TILE * TILE), BF16),
        pltpu.VMEM((2, 32, 128), F32),
        pltpu.VMEM((17, 32, 128), F32),
        pltpu.VMEM((TILE, 128), F32),
        pltpu.VMEM(pairs, F32),
        pltpu.VMEM(pairs, F32),
        pltpu.VMEM((4, 3 * TILE, 128), F32),
        pltpu.VMEM((4,) + pairs, F32),
        pltpu.VMEM((H,) + pairs, BF16),
        pltpu.VMEM((H,) + pairs, BF16),
        pltpu.VMEM((H,) + pairs, BF16),
        pltpu.VMEM((H,) + pairs, BF16),
        pltpu.VMEM((8, 16, 128), BF16),
        pltpu.VMEM((Y, UP, 16, 128), BF16),
        pltpu.VMEM((XS, UP, 16, 128), F32),
        pltpu.VMEM((2, XS, PAIRS, ZS, 16, 128), BF16),
        pltpu.VMEM((KB * 128, width // 2), BF16),
        pltpu.VMEM((tokens, width), F32),
        pltpu.VMEM((17, 32, 128), F32),
        pltpu.VMEM(fine.shape, BF16),
        pltpu.VMEM(rows_low.shape, BF16),
        pltpu.VMEM(cols_low.shape, BF16),
        pltpu.SMEM((1, 8), jnp.int32),
        pltpu.SMEM((1, 1), jnp.int32),
        dma((10,)), dma((Z,)), dma((Z,)), dma(()), dma(()),
        dma((H, 2)), dma((H, 2)), dma((H, 2)), dma((H, 2)),
        *spread_sems, *spread_sems,
        dma((Y,)), dma((Y,)), dma((XS,)), dma((XS,)), dma(()),
    ]
    values, new_momentum = pl.pallas_call(
        functools.partial(kernel, Y, Z, scale),
        out_shape=(
            jax.ShapeDtypeStruct((tokens, width), BF16),
            jax.ShapeDtypeStruct((15, 32, 128), F32),
        ),
        in_specs=[hbm] * 10,
        out_specs=(vmem, hbm),
        scratch_shapes=scratch,
        compiler_params=pltpu.CompilerParams(
            collective_id=0, has_side_effects=True, vmem_limit_bytes=60 * 1024 * 1024),
        cost_estimate=pl.CostEstimate(
            flops=4 * tokens * depth * width, bytes_accessed=8 * tokens * depth, transcendentals=0),
    )(
        activations.T, cotangent, next_inputs.T, weight_tiles,
        momentum.reshape(15, 32, 128), chosen.reshape(1, 8), counts,
        jnp.asarray(fine), jnp.asarray(rows_low), jnp.asarray(cols_low),
    )
    return values, new_momentum.reshape(1, 15, TILE * TILE)


def solution(mesh):
    Y, Z = mesh.shape["replica"] // XS, mesh.shape["tok"] // 2
    return jax.shard_map(
        functools.partial(local, Y, Z),
        mesh=mesh,
        in_specs=(
            P(("replica", "tok"), None),
            P(("replica", "tok"), None),
            P(("replica", "tok"), None),
            P("tok", None),
            P("replica", "tok", None),
            P("replica", "tok", None),
            P("replica", "tok"),
        ),
        out_specs=(P(("replica", "tok"), None), P("replica", "tok", None)),
        check_vma=False,
    )
```

```python
import functools
import math

import jax
import jax.numpy as jnp
import numpy as np
from jax import lax
from jax.experimental import pallas as pl
from jax.experimental.pallas import tpu as pltpu
from jax.sharding import PartitionSpec as P

TILE = 64
KEEP = 32
CHIP_TILES = 30
CHIP_PAIRS = 15
PAIRS = 8
XS = 4

momentum_decay = 0.9
step_size = 0.01
F32 = jnp.float32
BF16 = jnp.bfloat16


def cosine_table():
    frequency = np.arange(KEEP)[:, None]
    position = np.arange(TILE)[None, :]
    cosines = np.cos(math.pi * (2.0 * position + 1.0) * frequency / (2.0 * TILE))
    factor = np.where(frequency == 0, math.sqrt(1.0 / TILE), math.sqrt(2.0 / TILE))
    return (cosines * factor).astype(np.float32)


def split(values):
    high = values.astype(jnp.bfloat16)
    return high, (values - high.astype(jnp.float32)).astype(jnp.bfloat16)


def tables(col_tiles):
    low = cosine_table()
    high_part, low_part = (np.asarray(v, np.float32) for v in split(low))
    two = np.kron(np.eye(2, dtype=np.float32), low.T)
    twice = np.concatenate([two, two], axis=1)
    back = np.concatenate([two.T, np.zeros((64, 128), np.float32)], axis=0)
    fine = np.zeros((768, 128), np.float32)
    fine[0:32, 0:64] = fine[0:32, 64:128] = high_part
    fine[32:64, 0:64] = fine[32:64, 64:128] = low_part
    fine[64:128, 0:32] = fine[64:128, 32:64] = high_part.T
    fine[64:128, 64:96] = low_part.T
    fine[128:256], fine[384:512] = (np.asarray(v, np.float32) for v in split(twice))
    fine[256:384] = fine[128:256]
    fine[512:640], fine[640:768] = (np.asarray(v, np.float32) for v in split(back))
    rows_low = np.kron(np.eye(4, dtype=np.float32), low.T)
    cols_low = np.kron(np.eye(col_tiles, dtype=np.float32), low)
    return fine.astype(jnp.bfloat16), rows_low.astype(jnp.bfloat16), cols_low.astype(jnp.bfloat16)


def far_first(size):
    return sorted(range(1, size), key=lambda o: -min(o, size - o))


def fold_sources(z_size, doubles):
    made = [[] for _ in range(doubles)]
    for z in range(z_size):
        for c in range(2):
            first = CHIP_PAIRS * z + 7 * c
            for p in range(PAIRS):
                pair = first + p
                block = p // 2 if first % 2 == 0 else ((p + 1) // 2) % 4
                lo = 64 * (pair % 2)
                hi = lo + 64
                if c == 0 and p == 7:
                    hi -= 32
                if c == 1 and p == 0:
                    lo += 32
                made[pair // 2].append((c, z, block, lo, hi))
    joined = []
    for parts in made:
        blocks = {}
        for c, z, block, lo, hi in parts:
            old = blocks.get((c, z, block), (lo, hi))
            blocks[c, z, block] = (min(old[0], lo), max(old[1], hi))
        joined.append([(k, v) for k, v in blocks.items()])
    return joined


def kernel(
    Y, Z, scale,
    at_ref, cot_ref, xt_ref, w_ref, mom_ref, chosen_in, counts_in, fine_in, rl_in, cl_in,
    values_ref, newm_ref,
    a_own, c_own, a_sib, c_sib, xt, xr, low_in, wall, wmat, wfull, wfold, mfold, wpair, u0, grad, prod, own,
    send_p, send_m, got_p, got_m, pack, ys, xs, sall, smat, base, nfold,
    fine_ref, rl_ref, cl_ref, chosen_ref, counts_ref,
    load_sem, a_send, a_recv, c_send, c_recv,
    rp_send, rp_recv, rm_send, rm_recv,
    wz_send, wz_recv, wy_send, wy_recv, wx_send, wx_recv, wc_send, wc_recv,
    sz_send, sz_recv, sy_send, sy_recv, sx_send, sx_recv, sc_send, sc_recv,
    ry_send, ry_recv, rx_send, rx_recv, out_sem,
):
    H = Z // 2
    ZS = Z // XS
    UP = 2
    D = at_ref.shape[0]
    RT = D // TILE
    KB = xr.shape[1] // 256
    replica, tok = lax.axis_index("replica"), lax.axis_index("tok")
    y, x = replica // XS, replica % XS
    z, c = tok // 2, tok % 2
    group = lax.rem(y, 4)
    sib = (replica, z * 2 + (1 - c))

    def at_z(o):
        return (replica, lax.rem(z + o, Z) * 2 + c)

    def at_y(o):
        return (lax.rem(y + o, Y) * XS + x, tok)

    def at_x(o):
        return (y * XS + lax.rem(x + o, XS), tok)

    def rc(src, dst, ss, rs, dev):
        return pltpu.make_async_remote_copy(
            src_ref=src, dst_ref=dst, send_sem=ss, recv_sem=rs,
            device_id=dev, device_id_type=pl.DeviceIdType.MESH)

    def dot(a, b):
        return lax.dot_general(a, b, (((1,), (0,)), ((), ())), preferred_element_type=F32)

    loads = [
        pltpu.make_async_copy(cot_ref, c_own, load_sem.at[0]),
        pltpu.make_async_copy(at_ref, a_own, load_sem.at[1]),
        pltpu.make_async_copy(w_ref, wfull, load_sem.at[2]),
        pltpu.make_async_copy(mom_ref, mfold.at[pl.ds(1, 15)], load_sem.at[3]),
        pltpu.make_async_copy(xt_ref, xt.at[pl.ds(0, D)], load_sem.at[4]),
        pltpu.make_async_copy(fine_in, fine_ref, load_sem.at[5]),
        pltpu.make_async_copy(rl_in, rl_ref, load_sem.at[6]),
        pltpu.make_async_copy(cl_in, cl_ref, load_sem.at[7]),
        pltpu.make_async_copy(chosen_in, chosen_ref, load_sem.at[8]),
        pltpu.make_async_copy(counts_in, counts_ref, load_sem.at[9]),
    ]

    barrier = pltpu.get_barrier_semaphore()
    pl.semaphore_signal(barrier, inc=1, device_id=sib, device_id_type=pl.DeviceIdType.MESH)
    for o in range(1, Z):
        pl.semaphore_signal(barrier, inc=1, device_id=at_z(o), device_id_type=pl.DeviceIdType.MESH)
    for o in range(1, Y):
        pl.semaphore_signal(barrier, inc=1, device_id=at_y(o), device_id_type=pl.DeviceIdType.MESH)
    for o in range(1, XS):
        pl.semaphore_signal(barrier, inc=1, device_id=at_x(o), device_id_type=pl.DeviceIdType.MESH)
    for load in loads:
        load.start()

    lane = lax.broadcasted_iota(jnp.int32, (32, 128), 1)
    left = lane < 64

    mfold[0] = jnp.zeros((32, 128), F32)
    mfold[16] = jnp.zeros((32, 128), F32)
    got_p[0, 4:8] = jnp.zeros((4, TILE, 128), BF16)
    got_m[0, 0:4] = jnp.zeros((4, TILE, 128), BF16)
    if KB * 256 > D:
        xt[D:, :] = jnp.zeros((KB * 256 - D, xt.shape[1]), BF16)
        wmat[D:, :] = jnp.zeros((KB * 256 - D, wmat.shape[1]), BF16)
        smat[D // 2:, :] = jnp.zeros((KB * 128 - D // 2, smat.shape[1]), BF16)

    pl.semaphore_wait(barrier, Z + Y + XS - 2)

    def row_start(e, core):
        dest = (z + e) % Z
        return jnp.minimum((CHIP_PAIRS * dest + 7 * core) // 4, RT - 3) * TILE

    def a_copy(e):
        rows = pl.ds(pl.multiple_of(row_start(e, 1 - c), TILE), 3 * TILE)
        return rc(at_ref.at[rows], a_sib.at[e], a_send.at[e], a_recv.at[e], sib)

    c_copy = rc(cot_ref, c_sib, c_send, c_recv, sib)
    c_copy.start()
    a_copy(H).start()

    @pl.loop(1, H)
    def _(s):
        a_copy(H - s).start()
        a_copy(H + s).start()

    a_copy(0).start()

    class Spread:
        def __init__(self, buf, zs_, zr, ys_, yr, xs_, xr_, cs, cr):
            self.buf, self.zs, self.zr, self.ys, self.yr = buf, zs_, zr, ys_, yr
            self.xs, self.xr, self.cs, self.cr = xs_, xr_, cs, cr

        def mine(self):
            return self.buf.at[c, x, pl.ds(UP * group, UP)]

        def z_copy(self, o):
            part = self.mine().at[:, z // XS]
            return rc(part, part, self.zs.at[o - 1], self.zr.at[z // XS], at_z(o))

        def start_z(self):
            @pl.when(z % XS == x)
            def _():
                for o in far_first(Z):
                    self.z_copy(o).start()

        def wait_z(self):
            @pl.loop(0, ZS)
            def _(k):
                @pl.when(z != x + XS * k)
                def _():
                    part = self.mine().at[:, k]
                    rc(part, part, self.zs.at[0], self.zr.at[k], at_z(1)).wait_recv()

        def y_copy(self, k):
            return rc(self.mine(), self.mine(), self.ys.at[k], self.yr.at[k], at_y((2, 1, Y - 1)[k]))

        def start_y(self):
            for k in range(3):
                self.y_copy(k).start()

        def wait_y(self):
            for k in range(3):
                source = lax.rem(group + (2, 3, 1)[k], 4)
                part = self.buf.at[c, x, pl.ds(UP * source, UP)]
                rc(part, part, self.ys.at[k], self.yr.at[k], at_y(1)).wait_recv()

        def x_copy(self, k):
            if k < 2:
                part = self.buf.at[c, x]
            else:
                near = (x + XS - 1) % XS if k == 2 else (x + 1) % XS
                part = self.buf.at[c, near, pl.ds(0 if k == 2 else 4, 4)]
            return rc(part, part, self.xs.at[k], self.xr.at[k], at_x(1 if k % 2 == 0 else XS - 1))

        def c_copy(self, k):
            part = self.buf.at[c, (x + k) % XS]
            return rc(part, part, self.cs.at[k], self.cr.at[k], sib)

        def start_x(self):
            self.x_copy(0).start()
            self.x_copy(1).start()
            self.c_copy(0).start()

        def forward_x(self):
            from_left = self.buf.at[c, (x + XS - 1) % XS]
            rc(from_left, from_left, self.xs.at[0], self.xr.at[0], at_x(1)).wait_recv()
            self.x_copy(2).start()
            self.c_copy(3).start()
            from_right = self.buf.at[c, (x + 1) % XS]
            rc(from_right, from_right, self.xs.at[1], self.xr.at[1], at_x(1)).wait_recv()
            self.x_copy(3).start()
            self.c_copy(1).start()

        def finish_x(self):
            far = (x + 2) % XS
            for k in (2, 3):
                part = self.buf.at[c, far, pl.ds(0 if k == 2 else 4, 4)]
                rc(part, part, self.xs.at[k], self.xr.at[k], at_x(1)).wait_recv()
            self.c_copy(2).start()

        def wait_core(self):
            for k in range(XS):
                part = self.buf.at[1 - c, (x + k) % XS]
                rc(part, part, self.cs.at[k], self.cr.at[k], sib).wait_recv()

        def wait_sends(self):
            @pl.when(z % XS == x)
            def _():
                @pl.loop(1, Z)
                def _(o):
                    self.z_copy(o).wait_send()

            for k in range(3):
                self.y_copy(k).wait_send()

            for k in range(4):
                self.x_copy(k).wait_send()
            for k in range(XS):
                self.c_copy(k).wait_send()

    wide = Spread(wall, wz_send, wz_recv, wy_send, wy_recv, wx_send, wx_recv, wc_send, wc_recv)
    quads = Spread(sall, sz_send, sz_recv, sy_send, sy_recv, sx_send, sx_recv, sc_send, sc_recv)

    def unfold(first, second):
        even = jnp.where(left, first, pltpu.roll(second, 64, 1))
        odd = jnp.where(left, pltpu.roll(first, 64, 1), second)
        return even, odd

    loads[0].wait()
    loads[1].wait()
    rc(c_sib, c_sib, c_send, c_recv, sib).wait_recv()

    def partial(e, slot):
        rc(a_sib.at[e], a_sib.at[e], a_send.at[e], a_recv.at[e], sib).wait_recv()
        start = row_start(e, c)
        rows = pl.ds(pl.multiple_of(start, TILE), 3 * TILE)
        total = dot(a_own[rows, :], c_own[...]) + dot(a_sib[e], c_sib[...])
        total = total * scale
        for j in range(4):
            prod[j] = total[:, 128 * j:128 * j + 128]
        first = CHIP_PAIRS * ((z + e) % Z) + 7 * c
        for p in range(PAIRS):
            pair = first + p
            row = pl.multiple_of((pair // 4) * TILE - start, TILE)
            own[slot, p] = prod[pair % 4, pl.ds(row, TILE), :]

    def p_copy(s, q):
        return rc(send_p.at[s, pl.ds(2 * q, 2)], got_p.at[s, pl.ds(2 * q, 2)],
                  rp_send.at[s, q], rp_recv.at[s, q], at_z(1))

    def m_copy(s, q):
        return rc(send_m.at[s, pl.ds(2 * q, 2)], got_m.at[s, pl.ds(2 * q, 2)],
                  rm_send.at[s, q], rm_recv.at[s, q], at_z(Z - 1))

    partial(H, 0)
    for k in range(2):
        send_p[0, 2 * k:2 * k + 2] = own[0, 2 * k:2 * k + 2].astype(BF16)
        p_copy(0, k).start()
        send_m[0, 2 * k + 4:2 * k + 6] = own[0, 2 * k + 4:2 * k + 6].astype(BF16)
        m_copy(0, k + 2).start()
    partial(H - 1, 2)
    partial(H + 1, 3)

    loads[2].wait()

    @pl.when(z % XS == x)
    def _():
        for k in range(UP):
            number = 2 * (UP * group + k) - c
            rows = lax.broadcasted_iota(jnp.int32, (15, 4096), 0)
            for tile in range(2):
                only = jnp.where(rows == number + tile, wfull[...].astype(F32), 0.0)
                only = jnp.sum(only, axis=0, keepdims=True)
                for r in range(32):
                    wfold[tile, r:r + 1, :] = only[:, 128 * r:128 * r + 128]
            even, odd = unfold(wfold[0], wfold[1])
            wpair[pl.ds(0, 32, stride=2), :] = even
            wpair[pl.ds(1, 32, stride=2), :] = odd
            wall[c, x, UP * group + k, z // XS] = wpair[...].astype(BF16)

    wide.start_z()

    @pl.loop(1, H)
    def _(s):
        now, later = 2 * (s % 2), 2 * ((s + 1) % 2)

        def pass_on(copy, got, send, slot, q, first):
            @pl.when(jnp.logical_or(s > 1, first))
            def _():
                copy(s - 1, q).wait_recv()

            part = own[slot, 2 * q:2 * q + 2] + got[s - 1, 2 * q:2 * q + 2].astype(F32)
            send[s, 2 * q:2 * q + 2] = part.astype(BF16)
            copy(s, q).start()

        for k in range(4):
            pass_on(p_copy, got_p, send_p, now, k, k < 2)
            pass_on(m_copy, got_m, send_m, now + 1, (k + 2) % 4, k < 2)
            if k == 1:
                partial(H - 1 - s, later)

        @pl.when(s < H - 1)
        def _():
            partial(H + 1 + s, later + 1)

        @pl.when(s == min(2, H - 1))
        def _():
            wide.wait_z()
            wide.start_y()

        @pl.when(s == min(5, H - 1))
        def _():
            wide.wait_y()
            wide.start_x()

    last = 2 * (H % 2)

    loads[3].wait()
    loads[5].wait()
    loads[8].wait()
    loads[9].wait()
    for p in range(PAIRS):
        even, odd = unfold(mfold[1 + 2 * p - c], mfold[2 + 2 * p - c])
        u0[p, pl.ds(0, 32, stride=2), :] = even * momentum_decay
        u0[p, pl.ds(1, 32, stride=2), :] = odd * momentum_decay
    for p in range(PAIRS):
        u0[p] = own[last, p] + u0[p]
    high, rest = split(jnp.concatenate([u0[p] for p in range(PAIRS)], axis=1))
    side_own = dot(fine_ref[0:64, 0:64], high)
    side_own = side_own[0:32] + side_own[32:64] + dot(fine_ref[0:32, 0:64], rest)

    shape = (PAIRS * KEEP, 128)
    number = 2 * (lax.broadcasted_iota(jnp.int32, shape, 0) // KEEP) - c
    number = number + (lax.broadcasted_iota(jnp.int32, shape, 1) // KEEP) % 2
    keep = jnp.zeros(shape, F32)
    for s in range(8):
        listed = jnp.where(s < counts_ref[0, 0], chosen_ref[0, s], -5)
        keep = jnp.where(number == listed, 1.0, keep)

    for q in range(4):
        p_copy(H - 1, q).wait_recv()
        m_copy(H - 1, q).wait_recv()
    arrived = jnp.concatenate(
        [jnp.concatenate([got[H - 1, p] for p in range(PAIRS)], axis=1) for got in (got_p, got_m)], axis=0)
    side = dot(fine_ref[0:64, :], arrived)
    side = side_own + (side[0:32] + side[32:64])
    side = jnp.concatenate([side[:, 128 * p:128 * p + 128] for p in range(PAIRS)], axis=0)
    high, rest = split(side)
    quad = dot(jnp.concatenate([high, rest, high], axis=1), fine_ref[128:512, :])
    quad = jnp.where(keep > 0.5, quad, 0.0).astype(BF16).astype(F32)
    odd_first = ((z + c) % 2) == 1
    for d in range(4):
        blocks = [quad[32 * p:32 * p + 32] for p in range(PAIRS)]
        plain = jnp.where(left, blocks[2 * d], blocks[2 * d + 1])
        turned = jnp.where(left, blocks[(2 * d + 7) % 8], blocks[2 * d])
        block = jnp.where(odd_first, turned, plain).astype(BF16)
        pack[2 * d] = block[0:16]
        pack[2 * d + 1] = block[16:32]

    def ry_copy(o):
        return rc(pack.at[pl.ds(UP * lax.rem(lax.rem(y + o, Y), 4), UP)], ys.at[o - 1],
                  ry_send.at[o - 1], ry_recv.at[o - 1], at_y(o))

    for o in far_first(Y):
        ry_copy(o).start()

    @pl.loop(1, Y)
    def _(o):
        ry_copy(o).wait_recv()

    total = pack[pl.ds(UP * group, UP)].astype(F32)
    for o in range(1, Y):
        total = total + ys[o - 1].astype(F32)
    xs[0] = total

    def rx_copy(o):
        return rc(xs.at[0], xs.at[o], rx_send.at[o - 1], rx_recv.at[o - 1], at_x(o))

    for o in far_first(XS):
        rx_copy(o).start()

    exact = quad.astype(BF16)
    quad_side = dot(jnp.concatenate([exact, exact], axis=1), fine_ref[512:768, :])
    quad_side = jnp.concatenate([quad_side[32 * p:32 * p + 32] for p in range(PAIRS)], axis=1)
    high, rest = split(quad_side)
    shift = dot(fine_ref[64:128, 0:96], jnp.concatenate([high, rest, high], axis=0))
    for p in range(PAIRS):
        got = got_p[H - 1, p].astype(F32) + got_m[H - 1, p].astype(F32)
        grad[p] = (u0[p] + got) - shift[:, 128 * p:128 * p + 128]

    for o in range(1, XS):
        rx_copy(o).wait_recv()
    total = (xs[0] + xs[2]) + (xs[1] + xs[3])

    @pl.when(z % XS == x)
    def _():
        for k in range(UP):
            sall[c, x, UP * group + k, z // XS] = total[k].astype(BF16)

    quads.start_z()

    for p in range(PAIRS):
        even = grad[p, pl.ds(0, 32, stride=2), :]
        odd = grad[p, pl.ds(1, 32, stride=2), :]
        nfold[1 + 2 * p - c] = jnp.where(left, even, pltpu.roll(odd, 64, 1))
        nfold[2 + 2 * p - c] = jnp.where(left, pltpu.roll(even, 64, 1), odd)
    out_copy = pltpu.make_async_copy(nfold.at[pl.ds(1, 15)], newm_ref, out_sem)
    out_copy.start()

    wide.forward_x()
    quads.wait_z()
    quads.start_y()
    loads[4].wait()
    loads[6].wait()
    loads[7].wait()

    @pl.loop(0, KB)
    def _(k):
        rows = pl.ds(pl.multiple_of(256 * k, 256), 256)
        xr[:, rows] = xt[rows, :].T

    quads.wait_y()
    quads.start_x()

    @pl.loop(0, KB)
    def _(k):
        rows = pl.ds(pl.multiple_of(256 * k, 256), 256)
        low_in[:, pl.ds(pl.multiple_of(128 * k, 128), 128)] = dot(xr[:, rows], rl_ref[...]).astype(BF16)

    wide.finish_x()
    wide.wait_core()
    left64 = lax.broadcasted_iota(jnp.int32, (TILE, 128), 1) < 64
    for zz in range(Z):
        for p in range(CHIP_PAIRS):
            pair = CHIP_PAIRS * zz + p
            core, slot = (0, p) if p < 8 else (1, p - 7)
            block = wall[core, zz % XS, slot, zz // XS]
            if p == 7:
                block = jnp.where(left64, block, wall[1, zz % XS, 0, zz // XS])
            wmat[TILE * (pair // 4):TILE * (pair // 4) + TILE,
                 128 * (pair % 4):128 * (pair % 4) + 128] = block

    quads.forward_x()
    base[...] = jnp.zeros(base.shape, F32)

    @pl.loop(0, KB)
    def _(k):
        rows = pl.ds(pl.multiple_of(256 * k, 256), 256)
        base[...] += dot(xr[:, rows], wmat[rows, :])

    quads.finish_x()
    quads.wait_core()

    lane16 = lax.broadcasted_iota(jnp.int32, (16, 128), 1)
    for n, parts in enumerate(fold_sources(Z, D * 2 // 64)):
        for half in range(2):
            block = None
            for (core, zz, d), (lo, hi) in parts:
                part = sall[core, zz % XS, 2 * d + half, zz // XS]
                if block is None:
                    block = part
                else:
                    block = jnp.where((lane16 >= lo) & (lane16 < hi), part, block)
            row = 32 * (n // 2) + 16 * half
            smat[row:row + 16, 128 * (n % 2):128 * (n % 2) + 128] = block

    late = dot(low_in[...], smat[...]) * step_size
    values_ref[...] = (base[...] - dot(late.astype(BF16), cl_ref[...])).astype(BF16)

    out_copy.wait()
    c_copy.wait_send()

    @pl.loop(0, Z)
    def _(e):
        a_copy(e).wait_send()

    for k in range(2):
        p_copy(0, k).wait_send()
        m_copy(0, k + 2).wait_send()

    @pl.loop(1, H)
    def _(s):
        for q in range(4):
            p_copy(s, q).wait_send()
            m_copy(s, q).wait_send()

    @pl.loop(1, Y)
    def _(o):
        ry_copy(o).wait_send()

    for o in range(1, XS):
        rx_copy(o).wait_send()
    wide.wait_sends()
    quads.wait_sends()


def hand_over(values_ref, newm_ref, values_out, newm_out, values_here, newm_here, sems):
    moves = ((values_ref, values_here, values_out), (newm_ref, newm_here, newm_out))
    fetched = [pltpu.make_async_copy(a, b, sems.at[k]) for k, (a, b, _) in enumerate(moves)]
    stored = [pltpu.make_async_copy(b, d, sems.at[2 + k]) for k, (_, b, d) in enumerate(moves)]
    for copy in fetched:
        copy.start()
    for before, copy in zip(fetched, stored):
        before.wait()
        copy.start()
    for copy in stored:
        copy.wait()


def local(Y, Z, activations, cotangent, next_inputs, weight_tiles, momentum, chosen, counts):
    tokens, depth = activations.shape
    width = cotangent.shape[1]
    scale = 1.0 / math.sqrt(tokens * 2 * Z)
    H, ZS, UP = Z // 2, Z // XS, 2
    KB = -(-depth // 256)
    fine, rows_low, cols_low = tables(width // TILE)
    hbm = pl.BlockSpec(memory_space=pl.ANY)
    vmem = pl.BlockSpec(memory_space=pltpu.VMEM)
    dma = pltpu.SemaphoreType.DMA
    spread_sems = [dma((Z - 1,)), dma((ZS,)), dma((Y,)), dma((Y,)), dma((4,)), dma((4,)), dma((4,)), dma((4,))]
    pairs = (PAIRS, TILE, 128)
    scratch = [
        pltpu.VMEM((depth, tokens), BF16),
        pltpu.VMEM((tokens, width), BF16),
        pltpu.VMEM((Z, 3 * TILE, tokens), BF16),
        pltpu.VMEM((tokens, width), BF16),
        pltpu.VMEM((KB * 256, tokens), BF16),
        pltpu.VMEM((tokens, KB * 256), BF16),
        pltpu.VMEM((tokens, KB * 128), BF16),
        pltpu.VMEM((2, XS, PAIRS, ZS, TILE, 128), BF16),
        pltpu.VMEM((KB * 256, width), BF16),
        pltpu.VMEM((15, TILE * TILE), BF16),
        pltpu.VMEM((2, 32, 128), F32),
        pltpu.VMEM((17, 32, 128), F32),
        pltpu.VMEM((TILE, 128), F32),
        pltpu.VMEM(pairs, F32),
        pltpu.VMEM(pairs, F32),
        pltpu.VMEM((4, 3 * TILE, 128), F32),
        pltpu.VMEM((4,) + pairs, F32),
        pltpu.VMEM((H,) + pairs, BF16),
        pltpu.VMEM((H,) + pairs, BF16),
        pltpu.VMEM((H,) + pairs, BF16),
        pltpu.VMEM((H,) + pairs, BF16),
        pltpu.VMEM((8, 16, 128), BF16),
        pltpu.VMEM((Y, UP, 16, 128), BF16),
        pltpu.VMEM((XS, UP, 16, 128), F32),
        pltpu.VMEM((2, XS, PAIRS, ZS, 16, 128), BF16),
        pltpu.VMEM((KB * 128, width // 2), BF16),
        pltpu.VMEM((tokens, width), F32),
        pltpu.VMEM((17, 32, 128), F32),
        pltpu.VMEM(fine.shape, BF16),
        pltpu.VMEM(rows_low.shape, BF16),
        pltpu.VMEM(cols_low.shape, BF16),
        pltpu.SMEM((1, 8), jnp.int32),
        pltpu.SMEM((1, 1), jnp.int32),
        dma((10,)), dma((Z,)), dma((Z,)), dma(()), dma(()),
        dma((H, 4)), dma((H, 4)), dma((H, 4)), dma((H, 4)),
        *spread_sems, *spread_sems,
        dma((Y,)), dma((Y,)), dma((XS,)), dma((XS,)), dma(()),
    ]
    values, new_momentum = pl.pallas_call(
        functools.partial(kernel, Y, Z, scale),
        out_shape=(
            jax.ShapeDtypeStruct((tokens, width), BF16),
            jax.ShapeDtypeStruct((15, 32, 128), F32),
        ),
        in_specs=[hbm] * 10,
        out_specs=(vmem, hbm),
        scratch_shapes=scratch,
        compiler_params=pltpu.CompilerParams(
            collective_id=0, has_side_effects=True, vmem_limit_bytes=60 * 1024 * 1024),
        cost_estimate=pl.CostEstimate(
            flops=4 * tokens * depth * width, bytes_accessed=8 * tokens * depth, transcendentals=0),
    )(
        activations.T, cotangent, next_inputs.T, weight_tiles,
        momentum.reshape(15, 32, 128), chosen.reshape(1, 8), counts,
        jnp.asarray(fine), jnp.asarray(rows_low), jnp.asarray(cols_low),
    )
    values, new_momentum = pl.pallas_call(
        hand_over,
        out_shape=(
            jax.ShapeDtypeStruct(values.shape, values.dtype),
            jax.ShapeDtypeStruct(new_momentum.shape, new_momentum.dtype),
        ),
        in_specs=[hbm, hbm],
        out_specs=(hbm, hbm),
        scratch_shapes=[pltpu.VMEM(values.shape, BF16), pltpu.VMEM(new_momentum.shape, F32), dma((4,))],
        compiler_params=pltpu.CompilerParams(vmem_limit_bytes=60 * 1024 * 1024),
    )(values, new_momentum)
    return values, new_momentum.reshape(1, 15, TILE * TILE)


def solution(mesh):
    Y, Z = mesh.shape["replica"] // XS, mesh.shape["tok"] // 2
    return jax.shard_map(
        functools.partial(local, Y, Z),
        mesh=mesh,
        in_specs=(
            P(("replica", "tok"), None),
            P(("replica", "tok"), None),
            P(("replica", "tok"), None),
            P("tok", None),
            P("replica", "tok", None),
            P("replica", "tok", None),
            P("replica", "tok"),
        ),
        out_specs=(P(("replica", "tok"), None), P("replica", "tok", None)),
        check_vma=False,
    )
```

```python
import functools
import math

import jax
import jax.numpy as jnp
import numpy as np
from jax import lax
from jax.experimental import pallas as pl
from jax.experimental.pallas import tpu as pltpu
from jax.sharding import PartitionSpec as P

TILE = 64
KEEP = 32
CHIP_TILES = 30
CHIP_PAIRS = 15
PAIRS = 8
XS = 4

momentum_decay = 0.9
step_size = 0.01
F32 = jnp.float32
BF16 = jnp.bfloat16


def cosine_table():
    frequency = np.arange(KEEP)[:, None]
    position = np.arange(TILE)[None, :]
    cosines = np.cos(math.pi * (2.0 * position + 1.0) * frequency / (2.0 * TILE))
    factor = np.where(frequency == 0, math.sqrt(1.0 / TILE), math.sqrt(2.0 / TILE))
    return (cosines * factor).astype(np.float32)


def split(values):
    high = values.astype(jnp.bfloat16)
    return high, (values - high.astype(jnp.float32)).astype(jnp.bfloat16)


def tables(col_tiles):
    low = cosine_table()
    high_part, low_part = (np.asarray(v, np.float32) for v in split(low))
    two = np.kron(np.eye(2, dtype=np.float32), low.T)
    twice = np.concatenate([two, two], axis=1)
    back = np.concatenate([two.T, np.zeros((64, 128), np.float32)], axis=0)
    fine = np.zeros((768, 128), np.float32)
    fine[0:32, 0:64] = fine[0:32, 64:128] = high_part
    fine[32:64, 0:64] = fine[32:64, 64:128] = low_part
    fine[64:128, 0:32] = fine[64:128, 32:64] = high_part.T
    fine[64:128, 64:96] = low_part.T
    fine[128:256], fine[384:512] = (np.asarray(v, np.float32) for v in split(twice))
    fine[256:384] = fine[128:256]
    fine[512:640], fine[640:768] = (np.asarray(v, np.float32) for v in split(back))
    rows_low = np.kron(np.eye(4, dtype=np.float32), low.T)
    cols_low = np.kron(np.eye(col_tiles, dtype=np.float32), low)
    return fine.astype(jnp.bfloat16), rows_low.astype(jnp.bfloat16), cols_low.astype(jnp.bfloat16)


def far_first(size):
    return sorted(range(1, size), key=lambda o: -min(o, size - o))


def fold_sources(z_size, doubles):
    made = [[] for _ in range(doubles)]
    for z in range(z_size):
        for c in range(2):
            first = CHIP_PAIRS * z + 7 * c
            for p in range(PAIRS):
                pair = first + p
                block = p // 2 if first % 2 == 0 else ((p + 1) // 2) % 4
                lo = 64 * (pair % 2)
                hi = lo + 64
                if c == 0 and p == 7:
                    hi -= 32
                if c == 1 and p == 0:
                    lo += 32
                made[pair // 2].append((c, z, block, lo, hi))
    joined = []
    for parts in made:
        blocks = {}
        for c, z, block, lo, hi in parts:
            old = blocks.get((c, z, block), (lo, hi))
            blocks[c, z, block] = (min(old[0], lo), max(old[1], hi))
        joined.append([(k, v) for k, v in blocks.items()])
    return joined


def kernel(
    Y, Z, scale,
    at_ref, cot_ref, xt_ref, w_ref, mom_ref, chosen_in, counts_in, fine_in, rl_in, cl_in,
    values_ref, newm_ref,
    a_own, c_own, a_sib, c_sib, xt, xr, low_in, wall, wmat, wfull, wfold, mfold, wpair, u0, grad, prod, own,
    send_p, send_m, got_p, got_m, pack, ys, xs, sall, smat, base, nfold,
    fine_ref, rl_ref, cl_ref, chosen_ref, counts_ref,
    load_sem, a_send, a_recv, c_send, c_recv,
    rp_send, rp_recv, rm_send, rm_recv,
    wz_send, wz_recv, wy_send, wy_recv, wx_send, wx_recv, wc_send, wc_recv,
    sz_send, sz_recv, sy_send, sy_recv, sx_send, sx_recv, sc_send, sc_recv,
    ry_send, ry_recv, rx_send, rx_recv, out_sem,
):
    H = Z // 2
    UP = 2
    D = at_ref.shape[0]
    RT = D // TILE
    KB = xr.shape[1] // 256
    replica, tok = lax.axis_index("replica"), lax.axis_index("tok")
    y, x = replica // XS, replica % XS
    z, c = tok // 2, tok % 2
    group = lax.rem(y, 4)
    sib = (replica, z * 2 + (1 - c))

    def at_z(o):
        return (replica, lax.rem(z + o, Z) * 2 + c)

    def at_y(o):
        return (lax.rem(y + o, Y) * XS + x, tok)

    def at_x(o):
        return (y * XS + lax.rem(x + o, XS), tok)

    def rc(src, dst, ss, rs, dev):
        return pltpu.make_async_remote_copy(
            src_ref=src, dst_ref=dst, send_sem=ss, recv_sem=rs,
            device_id=dev, device_id_type=pl.DeviceIdType.MESH)

    def dot(a, b):
        return lax.dot_general(a, b, (((1,), (0,)), ((), ())), preferred_element_type=F32)

    loads = [
        pltpu.make_async_copy(cot_ref, c_own, load_sem.at[0]),
        pltpu.make_async_copy(at_ref, a_own, load_sem.at[1]),
        pltpu.make_async_copy(w_ref, wfull, load_sem.at[2]),
        pltpu.make_async_copy(mom_ref, mfold.at[pl.ds(1, 15)], load_sem.at[3]),
        pltpu.make_async_copy(xt_ref, xt.at[pl.ds(0, D)], load_sem.at[4]),
        pltpu.make_async_copy(fine_in, fine_ref, load_sem.at[5]),
        pltpu.make_async_copy(rl_in, rl_ref, load_sem.at[6]),
        pltpu.make_async_copy(cl_in, cl_ref, load_sem.at[7]),
        pltpu.make_async_copy(chosen_in, chosen_ref, load_sem.at[8]),
        pltpu.make_async_copy(counts_in, counts_ref, load_sem.at[9]),
    ]

    barrier = pltpu.get_barrier_semaphore()
    pl.semaphore_signal(barrier, inc=1, device_id=sib, device_id_type=pl.DeviceIdType.MESH)
    for o in range(1, Z):
        pl.semaphore_signal(barrier, inc=1, device_id=at_z(o), device_id_type=pl.DeviceIdType.MESH)
    for o in range(1, Y):
        pl.semaphore_signal(barrier, inc=1, device_id=at_y(o), device_id_type=pl.DeviceIdType.MESH)
    for o in range(1, XS):
        pl.semaphore_signal(barrier, inc=1, device_id=at_x(o), device_id_type=pl.DeviceIdType.MESH)
    for load in loads:
        load.start()

    lane = lax.broadcasted_iota(jnp.int32, (32, 128), 1)
    left = lane < 64

    mfold[0] = jnp.zeros((32, 128), F32)
    mfold[16] = jnp.zeros((32, 128), F32)
    got_p[0, 4:8] = jnp.zeros((4, TILE, 128), BF16)
    got_m[0, 0:4] = jnp.zeros((4, TILE, 128), BF16)
    if KB * 256 > D:
        xt[D:, :] = jnp.zeros((KB * 256 - D, xt.shape[1]), BF16)
        wmat[D:, :] = jnp.zeros((KB * 256 - D, wmat.shape[1]), BF16)
        smat[D // 2:, :] = jnp.zeros((KB * 128 - D // 2, smat.shape[1]), BF16)

    class Spread:
        def __init__(self, buf, zs_, zr, ys_, yr, xs_, xr_, cs, cr):
            self.buf, self.zs, self.zr, self.ys, self.yr = buf, zs_, zr, ys_, yr
            self.xs, self.xr, self.cs, self.cr = xs_, xr_, cs, cr
            self.classes = buf.shape[1]
            self.side = lax.rem(x, self.classes)
            self.at_class = lax.rem(z, self.classes) == self.side

        def mine(self):
            return self.buf.at[c, self.side, pl.ds(UP * group, UP)]

        def z_copy(self, o):
            part = self.mine().at[:, z // self.classes]
            return rc(part, part, self.zs.at[o - 1], self.zr.at[z // self.classes], at_z(o))

        def start_z(self):
            @pl.when(self.at_class)
            def _():
                for o in far_first(Z):
                    self.z_copy(o).start()

        def wait_z(self):
            @pl.loop(0, Z // self.classes)
            def _(k):
                @pl.when(z != self.side + self.classes * k)
                def _():
                    part = self.mine().at[:, k]
                    rc(part, part, self.zs.at[0], self.zr.at[k], at_z(1)).wait_recv()

        def y_copy(self, k):
            return rc(self.mine(), self.mine(), self.ys.at[k], self.yr.at[k], at_y((2, 1, Y - 1)[k]))

        def start_y(self):
            for k in range(3):
                self.y_copy(k).start()

        def wait_y(self):
            for k in range(3):
                source = lax.rem(group + (2, 3, 1)[k], 4)
                part = self.buf.at[c, self.side, pl.ds(UP * source, UP)]
                rc(part, part, self.ys.at[k], self.yr.at[k], at_y(1)).wait_recv()

        def half(self, core, side, k):
            return self.buf.at[core, side, pl.ds(4 * k, 4)]

        def x_copy(self, k):
            if self.classes == 2:
                part = self.half(c, self.side, k)
            elif k < 2:
                part = self.buf.at[c, self.side]
            else:
                part = self.half(c, lax.rem(x + (XS - 1, 1)[k - 2], XS), k - 2)
            return rc(part, part, self.xs.at[k], self.xr.at[k], at_x((1, XS - 1)[k % 2]))

        def core_parts(self, core):
            if self.classes == 2:
                return [self.buf.at[core, self.side], self.half(core, 1 - self.side, 0), self.half(core, 1 - self.side, 1)]
            return [self.buf.at[core, lax.rem(x + o, XS)] for o in (0, XS - 1, 1, 2)]

        def c_copy(self, k):
            part = self.core_parts(c)[k]
            return rc(part, part, self.cs.at[k], self.cr.at[k], sib)

        def start_x(self):
            self.x_copy(0).start()
            self.x_copy(1).start()
            self.c_copy(0).start()

        def wait_x(self, part, k):
            rc(part, part, self.xs.at[k], self.xr.at[k], at_x(1)).wait_recv()

        def forward_x(self):
            for k in range(2):
                self.wait_x(self.buf.at[c, lax.rem(x + (XS - 1, 1)[k], XS)], k)
                self.x_copy(2 + k).start()
                self.c_copy(1 + k).start()

        def finish_x(self):
            for k in range(2):
                if self.classes == 2:
                    self.wait_x(self.half(c, 1 - self.side, k), k)
                    self.c_copy(1 + k).start()
                else:
                    self.wait_x(self.half(c, lax.rem(x + 2, XS), k), 2 + k)
            if self.classes == XS:
                self.c_copy(3).start()

        def wait_core(self):
            for k, part in enumerate(self.core_parts(1 - c)):
                rc(part, part, self.cs.at[k], self.cr.at[k], sib).wait_recv()

        def wait_sends(self):
            @pl.when(self.at_class)
            def _():
                @pl.loop(1, Z)
                def _(o):
                    self.z_copy(o).wait_send()

            for k in range(3):
                self.y_copy(k).wait_send()

            for k in range(2 if self.classes == 2 else 4):
                self.x_copy(k).wait_send()
            for k in range(len(self.core_parts(c))):
                self.c_copy(k).wait_send()

    wide = Spread(wall, wz_send, wz_recv, wy_send, wy_recv, wx_send, wx_recv, wc_send, wc_recv)
    quads = Spread(sall, sz_send, sz_recv, sy_send, sy_recv, sx_send, sx_recv, sc_send, sc_recv)

    def unfold(first, second):
        even = jnp.where(left, first, pltpu.roll(second, 64, 1))
        odd = jnp.where(left, pltpu.roll(first, 64, 1), second)
        return even, odd

    loads[2].wait()

    @pl.when(wide.at_class)
    def _():
        for k in range(UP):
            number = 2 * (UP * group + k) - c
            rows = lax.broadcasted_iota(jnp.int32, (15, 4096), 0)
            for tile in range(2):
                only = jnp.where(rows == number + tile, wfull[...].astype(F32), 0.0)
                only = jnp.sum(only, axis=0, keepdims=True)
                for r in range(32):
                    wfold[tile, r:r + 1, :] = only[:, 128 * r:128 * r + 128]
            even, odd = unfold(wfold[0], wfold[1])
            wpair[pl.ds(0, 32, stride=2), :] = even
            wpair[pl.ds(1, 32, stride=2), :] = odd
            wall[c, wide.side, UP * group + k, z // XS] = wpair[...].astype(BF16)

    pl.semaphore_wait(barrier, Z + Y + XS - 2)

    def row_start(e, core):
        dest = (z + e) % Z
        return jnp.minimum((CHIP_PAIRS * dest + 7 * core) // 4, RT - 3) * TILE

    def a_copy(e):
        rows = pl.ds(pl.multiple_of(row_start(e, 1 - c), TILE), 3 * TILE)
        return rc(at_ref.at[rows], a_sib.at[e], a_send.at[e], a_recv.at[e], sib)

    c_copy = rc(cot_ref, c_sib, c_send, c_recv, sib)
    c_copy.start()
    a_copy(H).start()

    a_copy(H - 1).start()
    a_copy(H + 1).start()

    loads[0].wait()
    loads[1].wait()
    rc(c_sib, c_sib, c_send, c_recv, sib).wait_recv()

    def partial(e, slot):
        rc(a_sib.at[e], a_sib.at[e], a_send.at[e], a_recv.at[e], sib).wait_recv()
        start = row_start(e, c)
        rows = pl.ds(pl.multiple_of(start, TILE), 3 * TILE)
        total = dot(a_own[rows, :], c_own[...]) + dot(a_sib[e], c_sib[...])
        total = total * scale
        for j in range(4):
            prod[j] = total[:, 128 * j:128 * j + 128]
        first = CHIP_PAIRS * ((z + e) % Z) + 7 * c
        for p in range(PAIRS):
            pair = first + p
            row = pl.multiple_of((pair // 4) * TILE - start, TILE)
            own[slot, p] = prod[pair % 4, pl.ds(row, TILE), :]

    def p_copy(s, q):
        return rc(send_p.at[s, pl.ds(2 * q, 2)], got_p.at[s, pl.ds(2 * q, 2)],
                  rp_send.at[s, q], rp_recv.at[s, q], at_z(1))

    def m_copy(s, q):
        return rc(send_m.at[s, pl.ds(2 * q, 2)], got_m.at[s, pl.ds(2 * q, 2)],
                  rm_send.at[s, q], rm_recv.at[s, q], at_z(Z - 1))

    partial(H, 0)
    for k in range(2):
        send_p[0, 2 * k:2 * k + 2] = own[0, 2 * k:2 * k + 2].astype(BF16)
        p_copy(0, k).start()
        send_m[0, 2 * k + 4:2 * k + 6] = own[0, 2 * k + 4:2 * k + 6].astype(BF16)
        m_copy(0, k + 2).start()

    @pl.loop(2, H)
    def _(s):
        a_copy(H - s).start()
        a_copy(H + s).start()

    a_copy(0).start()
    partial(H - 1, 2)
    partial(H + 1, 3)

    wide.start_z()

    @pl.loop(1, H)
    def _(s):
        now, later = 2 * (s % 2), 2 * ((s + 1) % 2)

        def pass_on(copy, got, send, slot, q, first):
            @pl.when(jnp.logical_or(s > 1, first))
            def _():
                copy(s - 1, q).wait_recv()

            part = own[slot, 2 * q:2 * q + 2] + got[s - 1, 2 * q:2 * q + 2].astype(F32)
            send[s, 2 * q:2 * q + 2] = part.astype(BF16)
            copy(s, q).start()

        for k in range(4):
            pass_on(p_copy, got_p, send_p, now, k, k < 2)
            pass_on(m_copy, got_m, send_m, now + 1, (k + 2) % 4, k < 2)
            if k == 1:
                partial(H - 1 - s, later)

        @pl.when(s < H - 1)
        def _():
            partial(H + 1 + s, later + 1)

        @pl.when(s == min(2, H - 1))
        def _():
            wide.wait_z()
            wide.start_y()

    last = 2 * (H % 2)

    loads[3].wait()
    loads[5].wait()
    loads[8].wait()
    loads[9].wait()
    for p in range(PAIRS):
        even, odd = unfold(mfold[1 + 2 * p - c], mfold[2 + 2 * p - c])
        u0[p, pl.ds(0, 32, stride=2), :] = even * momentum_decay
        u0[p, pl.ds(1, 32, stride=2), :] = odd * momentum_decay
    for p in range(PAIRS):
        u0[p] = own[last, p] + u0[p]
    high, rest = split(jnp.concatenate([u0[p] for p in range(PAIRS)], axis=1))
    side_own = dot(fine_ref[0:64, 0:64], high)
    side_own = side_own[0:32] + side_own[32:64] + dot(fine_ref[0:32, 0:64], rest)

    shape = (PAIRS * KEEP, 128)
    number = 2 * (lax.broadcasted_iota(jnp.int32, shape, 0) // KEEP) - c
    number = number + (lax.broadcasted_iota(jnp.int32, shape, 1) // KEEP) % 2
    keep = jnp.zeros(shape, F32)
    for s in range(8):
        listed = jnp.where(s < counts_ref[0, 0], chosen_ref[0, s], -5)
        keep = jnp.where(number == listed, 1.0, keep)

    wide.wait_y()
    wide.start_x()
    for q in range(4):
        p_copy(H - 1, q).wait_recv()
        m_copy(H - 1, q).wait_recv()
    arrived = jnp.concatenate(
        [jnp.concatenate([got[H - 1, p] for p in range(PAIRS)], axis=1) for got in (got_p, got_m)], axis=0)
    side = dot(fine_ref[0:64, :], arrived)
    side = side_own + (side[0:32] + side[32:64])
    side = jnp.concatenate([side[:, 128 * p:128 * p + 128] for p in range(PAIRS)], axis=0)
    high, rest = split(side)
    quad = dot(jnp.concatenate([high, rest, high], axis=1), fine_ref[128:512, :])
    quad = jnp.where(keep > 0.5, quad, 0.0).astype(BF16).astype(F32)
    odd_first = ((z + c) % 2) == 1
    for d in range(4):
        blocks = [quad[32 * p:32 * p + 32] for p in range(PAIRS)]
        plain = jnp.where(left, blocks[2 * d], blocks[2 * d + 1])
        turned = jnp.where(left, blocks[(2 * d + 7) % 8], blocks[2 * d])
        block = jnp.where(odd_first, turned, plain).astype(BF16)
        pack[2 * d] = block[0:16]
        pack[2 * d + 1] = block[16:32]

    def ry_copy(o):
        return rc(pack.at[pl.ds(UP * lax.rem(lax.rem(y + o, Y), 4), UP)], ys.at[o - 1],
                  ry_send.at[o - 1], ry_recv.at[o - 1], at_y(o))

    for o in far_first(Y):
        ry_copy(o).start()

    @pl.loop(1, Y)
    def _(o):
        ry_copy(o).wait_recv()

    total = pack[pl.ds(UP * group, UP)].astype(F32)
    for o in range(1, Y):
        total = total + ys[o - 1].astype(F32)
    xs[0] = total

    def rx_copy(o):
        return rc(xs.at[0], xs.at[o], rx_send.at[o - 1], rx_recv.at[o - 1], at_x(o))

    for o in far_first(XS):
        rx_copy(o).start()

    exact = quad.astype(BF16)
    quad_side = dot(jnp.concatenate([exact, exact], axis=1), fine_ref[512:768, :])
    quad_side = jnp.concatenate([quad_side[32 * p:32 * p + 32] for p in range(PAIRS)], axis=1)
    high, rest = split(quad_side)
    shift = dot(fine_ref[64:128, 0:96], jnp.concatenate([high, rest, high], axis=0))
    for p in range(PAIRS):
        got = got_p[H - 1, p].astype(F32) + got_m[H - 1, p].astype(F32)
        grad[p] = (u0[p] + got) - shift[:, 128 * p:128 * p + 128]

    for o in range(1, XS):
        rx_copy(o).wait_recv()
    total = (xs[0] + xs[2]) + (xs[1] + xs[3])

    @pl.when(quads.at_class)
    def _():
        for k in range(UP):
            sall[c, quads.side, UP * group + k, z // 2] = total[k].astype(BF16)

    quads.start_z()

    for p in range(PAIRS):
        even = grad[p, pl.ds(0, 32, stride=2), :]
        odd = grad[p, pl.ds(1, 32, stride=2), :]
        nfold[1 + 2 * p - c] = jnp.where(left, even, pltpu.roll(odd, 64, 1))
        nfold[2 + 2 * p - c] = jnp.where(left, pltpu.roll(even, 64, 1), odd)
    out_copy = pltpu.make_async_copy(nfold.at[pl.ds(1, 15)], newm_ref, out_sem)
    out_copy.start()

    wide.forward_x()
    quads.wait_z()
    quads.start_y()
    loads[4].wait()
    loads[6].wait()
    loads[7].wait()

    @pl.loop(0, KB)
    def _(k):
        rows = pl.ds(pl.multiple_of(256 * k, 256), 256)
        xr[:, rows] = xt[rows, :].T

    quads.wait_y()
    quads.start_x()
    wide.finish_x()

    @pl.loop(0, KB)
    def _(k):
        rows = pl.ds(pl.multiple_of(256 * k, 256), 256)
        low_in[:, pl.ds(pl.multiple_of(128 * k, 128), 128)] = dot(xr[:, rows], rl_ref[...]).astype(BF16)

    wide.wait_core()
    left64 = lax.broadcasted_iota(jnp.int32, (TILE, 128), 1) < 64
    for zz in range(Z):
        for p in range(CHIP_PAIRS):
            pair = CHIP_PAIRS * zz + p
            core, slot = (0, p) if p < 8 else (1, p - 7)
            block = wall[core, zz % XS, slot, zz // XS]
            if p == 7:
                block = jnp.where(left64, block, wall[1, zz % XS, 0, zz // XS])
            wmat[TILE * (pair // 4):TILE * (pair // 4) + TILE,
                 128 * (pair % 4):128 * (pair % 4) + 128] = block

    base[...] = jnp.zeros(base.shape, F32)

    @pl.loop(0, KB)
    def _(k):
        rows = pl.ds(pl.multiple_of(256 * k, 256), 256)
        base[...] += dot(xr[:, rows], wmat[rows, :])

    quads.finish_x()
    quads.wait_core()

    lane16 = lax.broadcasted_iota(jnp.int32, (16, 128), 1)
    for n, parts in enumerate(fold_sources(Z, D * 2 // 64)):
        for half in range(2):
            block = None
            for (core, zz, d), (lo, hi) in parts:
                part = sall[core, zz % 2, 2 * d + half, zz // 2]
                if block is None:
                    block = part
                else:
                    block = jnp.where((lane16 >= lo) & (lane16 < hi), part, block)
            row = 32 * (n // 2) + 16 * half
            smat[row:row + 16, 128 * (n % 2):128 * (n % 2) + 128] = block

    late = dot(low_in[...], smat[...]) * step_size
    values_ref[...] = (base[...] - dot(late.astype(BF16), cl_ref[...])).astype(BF16)

    out_copy.wait()
    c_copy.wait_send()

    @pl.loop(0, Z)
    def _(e):
        a_copy(e).wait_send()

    for k in range(2):
        p_copy(0, k).wait_send()
        m_copy(0, k + 2).wait_send()

    @pl.loop(1, H)
    def _(s):
        for q in range(4):
            p_copy(s, q).wait_send()
            m_copy(s, q).wait_send()

    @pl.loop(1, Y)
    def _(o):
        ry_copy(o).wait_send()

    for o in range(1, XS):
        rx_copy(o).wait_send()
    wide.wait_sends()
    quads.wait_sends()


def hand_over(values_ref, newm_ref, values_out, newm_out, values_here, newm_here, sems):
    moves = ((values_ref, values_here, values_out), (newm_ref, newm_here, newm_out))
    fetched = [pltpu.make_async_copy(a, b, sems.at[k]) for k, (a, b, _) in enumerate(moves)]
    stored = [pltpu.make_async_copy(b, d, sems.at[2 + k]) for k, (_, b, d) in enumerate(moves)]
    for copy in fetched:
        copy.start()
    for before, copy in zip(fetched, stored):
        before.wait()
        copy.start()
    for copy in stored:
        copy.wait()


def local(Y, Z, activations, cotangent, next_inputs, weight_tiles, momentum, chosen, counts):
    tokens, depth = activations.shape
    width = cotangent.shape[1]
    scale = 1.0 / math.sqrt(tokens * 2 * Z)
    H, UP = Z // 2, 2
    KB = -(-depth // 256)
    fine, rows_low, cols_low = tables(width // TILE)
    hbm = pl.BlockSpec(memory_space=pl.ANY)
    vmem = pl.BlockSpec(memory_space=pltpu.VMEM)
    dma = pltpu.SemaphoreType.DMA
    spread_sems = [dma((Z - 1,)), dma((Z // 2,)), dma((Y,)), dma((Y,)), dma((4,)), dma((4,)), dma((4,)), dma((4,))]
    pairs = (PAIRS, TILE, 128)
    scratch = [
        pltpu.VMEM((depth, tokens), BF16),
        pltpu.VMEM((tokens, width), BF16),
        pltpu.VMEM((Z, 3 * TILE, tokens), BF16),
        pltpu.VMEM((tokens, width), BF16),
        pltpu.VMEM((KB * 256, tokens), BF16),
        pltpu.VMEM((tokens, KB * 256), BF16),
        pltpu.VMEM((tokens, KB * 128), BF16),
        pltpu.VMEM((2, XS, PAIRS, Z // XS, TILE, 128), BF16),
        pltpu.VMEM((KB * 256, width), BF16),
        pltpu.VMEM((15, TILE * TILE), BF16),
        pltpu.VMEM((2, 32, 128), F32),
        pltpu.VMEM((17, 32, 128), F32),
        pltpu.VMEM((TILE, 128), F32),
        pltpu.VMEM(pairs, F32),
        pltpu.VMEM(pairs, F32),
        pltpu.VMEM((4, 3 * TILE, 128), F32),
        pltpu.VMEM((4,) + pairs, F32),
        pltpu.VMEM((H,) + pairs, BF16),
        pltpu.VMEM((H,) + pairs, BF16),
        pltpu.VMEM((H,) + pairs, BF16),
        pltpu.VMEM((H,) + pairs, BF16),
        pltpu.VMEM((8, 16, 128), BF16),
        pltpu.VMEM((Y, UP, 16, 128), BF16),
        pltpu.VMEM((XS, UP, 16, 128), F32),
        pltpu.VMEM((2, 2, PAIRS, Z // 2, 16, 128), BF16),
        pltpu.VMEM((KB * 128, width // 2), BF16),
        pltpu.VMEM((tokens, width), F32),
        pltpu.VMEM((17, 32, 128), F32),
        pltpu.VMEM(fine.shape, BF16),
        pltpu.VMEM(rows_low.shape, BF16),
        pltpu.VMEM(cols_low.shape, BF16),
        pltpu.SMEM((1, 8), jnp.int32),
        pltpu.SMEM((1, 1), jnp.int32),
        dma((10,)), dma((Z,)), dma((Z,)), dma(()), dma(()),
        dma((H, 4)), dma((H, 4)), dma((H, 4)), dma((H, 4)),
        *spread_sems, *spread_sems,
        dma((Y,)), dma((Y,)), dma((XS,)), dma((XS,)), dma(()),
    ]
    values, new_momentum = pl.pallas_call(
        functools.partial(kernel, Y, Z, scale),
        out_shape=(
            jax.ShapeDtypeStruct((tokens, width), BF16),
            jax.ShapeDtypeStruct((15, 32, 128), F32),
        ),
        in_specs=[hbm] * 10,
        out_specs=(vmem, hbm),
        scratch_shapes=scratch,
        compiler_params=pltpu.CompilerParams(
            collective_id=0, has_side_effects=True, vmem_limit_bytes=60 * 1024 * 1024),
        cost_estimate=pl.CostEstimate(
            flops=4 * tokens * depth * width, bytes_accessed=8 * tokens * depth, transcendentals=0),
    )(
        activations.T, cotangent, next_inputs.T, weight_tiles,
        momentum.reshape(15, 32, 128), chosen.reshape(1, 8), counts,
        jnp.asarray(fine), jnp.asarray(rows_low), jnp.asarray(cols_low),
    )
    values, new_momentum = pl.pallas_call(
        hand_over,
        out_shape=(
            jax.ShapeDtypeStruct(values.shape, values.dtype),
            jax.ShapeDtypeStruct(new_momentum.shape, new_momentum.dtype),
        ),
        in_specs=[hbm, hbm],
        out_specs=(hbm, hbm),
        scratch_shapes=[pltpu.VMEM(values.shape, BF16), pltpu.VMEM(new_momentum.shape, F32), dma((4,))],
        compiler_params=pltpu.CompilerParams(vmem_limit_bytes=60 * 1024 * 1024),
    )(values, new_momentum)
    return values, new_momentum.reshape(1, 15, TILE * TILE)


def solution(mesh):
    Y, Z = mesh.shape["replica"] // XS, mesh.shape["tok"] // 2
    return jax.shard_map(
        functools.partial(local, Y, Z),
        mesh=mesh,
        in_specs=(
            P(("replica", "tok"), None),
            P(("replica", "tok"), None),
            P(("replica", "tok"), None),
            P("tok", None),
            P("replica", "tok", None),
            P("replica", "tok", None),
            P("replica", "tok"),
        ),
        out_specs=(P(("replica", "tok"), None), P("replica", "tok", None)),
        check_vma=False,
    )
```

```python
import functools
import math

import jax
import jax.numpy as jnp
import numpy as np
from jax import lax
from jax.experimental import pallas as pl
from jax.experimental.pallas import tpu as pltpu
from jax.sharding import PartitionSpec as P

TILE = 64
KEEP = 32
CHIP_TILES = 30
CHIP_PAIRS = 15
PAIRS = 8
XS = 4

momentum_decay = 0.9
step_size = 0.01
F32 = jnp.float32
BF16 = jnp.bfloat16


def cosine_table():
    frequency = np.arange(KEEP)[:, None]
    position = np.arange(TILE)[None, :]
    cosines = np.cos(math.pi * (2.0 * position + 1.0) * frequency / (2.0 * TILE))
    factor = np.where(frequency == 0, math.sqrt(1.0 / TILE), math.sqrt(2.0 / TILE))
    return (cosines * factor).astype(np.float32)


def split(values):
    high = values.astype(jnp.bfloat16)
    return high, (values - high.astype(jnp.float32)).astype(jnp.bfloat16)


def tables(col_tiles):
    low = cosine_table()
    high_part, low_part = (np.asarray(v, np.float32) for v in split(low))
    two = np.kron(np.eye(2, dtype=np.float32), low.T)
    twice = np.concatenate([two, two], axis=1)
    back = np.concatenate([two.T, np.zeros((64, 128), np.float32)], axis=0)
    fine = np.zeros((768, 128), np.float32)
    fine[0:32, 0:64] = fine[0:32, 64:128] = high_part
    fine[32:64, 0:64] = fine[32:64, 64:128] = low_part
    fine[64:128, 0:32] = fine[64:128, 32:64] = high_part.T
    fine[64:128, 64:96] = low_part.T
    fine[128:256], fine[384:512] = (np.asarray(v, np.float32) for v in split(twice))
    fine[256:384] = fine[128:256]
    fine[512:640], fine[640:768] = (np.asarray(v, np.float32) for v in split(back))
    rows_low = np.kron(np.eye(4, dtype=np.float32), low.T)
    cols_low = np.kron(np.eye(col_tiles, dtype=np.float32), low)
    return fine.astype(jnp.bfloat16), rows_low.astype(jnp.bfloat16), cols_low.astype(jnp.bfloat16)


def far_first(size):
    return sorted(range(1, size), key=lambda o: -min(o, size - o))


def fold_sources(z_size, doubles):
    made = [[] for _ in range(doubles)]
    for z in range(z_size):
        for c in range(2):
            first = CHIP_PAIRS * z + 7 * c
            for p in range(PAIRS):
                pair = first + p
                block = p // 2 if first % 2 == 0 else ((p + 1) // 2) % 4
                lo = 64 * (pair % 2)
                hi = lo + 64
                if c == 0 and p == 7:
                    hi -= 32
                if c == 1 and p == 0:
                    lo += 32
                made[pair // 2].append((c, z, block, lo, hi))
    joined = []
    for parts in made:
        blocks = {}
        for c, z, block, lo, hi in parts:
            old = blocks.get((c, z, block), (lo, hi))
            blocks[c, z, block] = (min(old[0], lo), max(old[1], hi))
        joined.append([(k, v) for k, v in blocks.items()])
    return joined


def kernel(
    Y, Z, scale,
    at_ref, cot_ref, xt_ref, w_ref, mom_ref, chosen_in, counts_in, fine_in, rl_in, cl_in,
    values_ref, newm_ref,
    a_own, c_own, a_sib, c_sib, xt, xr, low_in, wall, wmat, wfull, wfold, mfold, wpair, u0, grad, prod, own,
    send_p, send_m, got_p, got_m, pack, ys, xs, sall, smat, base, nfold,
    fine_ref, rl_ref, cl_ref, chosen_ref, counts_ref,
    load_sem, a_send, a_recv, c_send, c_recv,
    rp_send, rp_recv, rm_send, rm_recv,
    wz_send, wz_recv, wy_send, wy_recv, wx_send, wx_recv, wc_send, wc_recv,
    sz_send, sz_recv, sy_send, sy_recv, sx_send, sx_recv, sc_send, sc_recv,
    ry_send, ry_recv, rx_send, rx_recv, out_sem,
):
    H = Z // 2
    UP = 2
    D = at_ref.shape[0]
    RT = D // TILE
    KB = xr.shape[1] // 256
    replica, tok = lax.axis_index("replica"), lax.axis_index("tok")
    y, x = replica // XS, replica % XS
    z, c = tok // 2, tok % 2
    group = lax.rem(y, 4)
    sib = (replica, z * 2 + (1 - c))

    def at_z(o):
        return (replica, lax.rem(z + o, Z) * 2 + c)

    def at_y(o):
        return (lax.rem(y + o, Y) * XS + x, tok)

    def at_x(o):
        return (y * XS + lax.rem(x + o, XS), tok)

    def rc(src, dst, ss, rs, dev):
        return pltpu.make_async_remote_copy(
            src_ref=src, dst_ref=dst, send_sem=ss, recv_sem=rs,
            device_id=dev, device_id_type=pl.DeviceIdType.MESH)

    def dot(a, b):
        return lax.dot_general(a, b, (((1,), (0,)), ((), ())), preferred_element_type=F32)

    loads = [
        pltpu.make_async_copy(cot_ref, c_own, load_sem.at[0]),
        pltpu.make_async_copy(at_ref, a_own, load_sem.at[1]),
        pltpu.make_async_copy(w_ref, wfull, load_sem.at[2]),
        pltpu.make_async_copy(mom_ref, mfold.at[pl.ds(1, 15)], load_sem.at[3]),
        pltpu.make_async_copy(xt_ref, xt.at[pl.ds(0, D)], load_sem.at[4]),
        pltpu.make_async_copy(fine_in, fine_ref, load_sem.at[5]),
        pltpu.make_async_copy(rl_in, rl_ref, load_sem.at[6]),
        pltpu.make_async_copy(cl_in, cl_ref, load_sem.at[7]),
        pltpu.make_async_copy(chosen_in, chosen_ref, load_sem.at[8]),
        pltpu.make_async_copy(counts_in, counts_ref, load_sem.at[9]),
    ]

    barrier = pltpu.get_barrier_semaphore()
    pl.semaphore_signal(barrier, inc=1, device_id=sib, device_id_type=pl.DeviceIdType.MESH)
    for o in range(1, Z):
        pl.semaphore_signal(barrier, inc=1, device_id=at_z(o), device_id_type=pl.DeviceIdType.MESH)
    for o in range(1, Y):
        pl.semaphore_signal(barrier, inc=1, device_id=at_y(o), device_id_type=pl.DeviceIdType.MESH)
    for o in range(1, XS):
        pl.semaphore_signal(barrier, inc=1, device_id=at_x(o), device_id_type=pl.DeviceIdType.MESH)
    for load in loads:
        load.start()

    lane = lax.broadcasted_iota(jnp.int32, (32, 128), 1)
    left = lane < 64

    mfold[0] = jnp.zeros((32, 128), F32)
    mfold[16] = jnp.zeros((32, 128), F32)
    got_p[0, 4:8] = jnp.zeros((4, TILE, 128), BF16)
    got_m[0, 0:4] = jnp.zeros((4, TILE, 128), BF16)
    if KB * 256 > D:
        xt[D:, :] = jnp.zeros((KB * 256 - D, xt.shape[1]), BF16)
        wmat[D:, :] = jnp.zeros((KB * 256 - D, wmat.shape[1]), BF16)
        smat[D // 2:, :] = jnp.zeros((KB * 128 - D // 2, smat.shape[1]), BF16)

    class Spread:
        def __init__(self, buf, zs_, zr, ys_, yr, xs_, xr_, cs, cr):
            self.buf, self.zs, self.zr, self.ys, self.yr = buf, zs_, zr, ys_, yr
            self.xs, self.xr, self.cs, self.cr = xs_, xr_, cs, cr
            self.classes = buf.shape[1]
            self.side = lax.rem(x, self.classes)
            self.at_class = lax.rem(z, self.classes) == self.side

        def mine(self):
            return self.buf.at[c, self.side, pl.ds(UP * group, UP)]

        def z_copy(self, o):
            part = self.mine().at[:, z // self.classes]
            return rc(part, part, self.zs.at[o - 1], self.zr.at[z // self.classes], at_z(o))

        def start_z(self):
            @pl.when(self.at_class)
            def _():
                for o in far_first(Z):
                    self.z_copy(o).start()

        def wait_z(self):
            @pl.loop(0, Z // self.classes)
            def _(k):
                @pl.when(z != self.side + self.classes * k)
                def _():
                    part = self.mine().at[:, k]
                    rc(part, part, self.zs.at[0], self.zr.at[k], at_z(1)).wait_recv()

        def y_copy(self, k):
            return rc(self.mine(), self.mine(), self.ys.at[k], self.yr.at[k], at_y((2, 1, Y - 1)[k]))

        def start_y(self):
            for k in range(3):
                self.y_copy(k).start()

        def wait_y(self):
            for k in range(3):
                source = lax.rem(group + (2, 3, 1)[k], 4)
                part = self.buf.at[c, self.side, pl.ds(UP * source, UP)]
                rc(part, part, self.ys.at[k], self.yr.at[k], at_y(1)).wait_recv()

        def half(self, core, side, k):
            return self.buf.at[core, side, pl.ds(4 * k, 4)]

        def x_copy(self, k):
            if self.classes == 2:
                part = self.half(c, self.side, k)
            elif k < 2:
                part = self.buf.at[c, self.side]
            else:
                part = self.half(c, lax.rem(x + (XS - 1, 1)[k - 2], XS), k - 2)
            return rc(part, part, self.xs.at[k], self.xr.at[k], at_x((1, XS - 1)[k % 2]))

        def core_parts(self, core):
            if self.classes == 2:
                return [self.buf.at[core, self.side], self.half(core, 1 - self.side, 0), self.half(core, 1 - self.side, 1)]
            return [self.buf.at[core, lax.rem(x + o, XS)] for o in (0, XS - 1, 1, 2)]

        def c_copy(self, k):
            part = self.core_parts(c)[k]
            return rc(part, part, self.cs.at[k], self.cr.at[k], sib)

        def start_x(self):
            self.x_copy(0).start()
            self.x_copy(1).start()
            self.c_copy(0).start()

        def wait_x(self, part, k):
            rc(part, part, self.xs.at[k], self.xr.at[k], at_x(1)).wait_recv()

        def forward_x(self):
            for k in range(2):
                self.wait_x(self.buf.at[c, lax.rem(x + (XS - 1, 1)[k], XS)], k)
                self.x_copy(2 + k).start()
                self.c_copy(1 + k).start()

        def finish_x(self):
            for k in range(2):
                if self.classes == 2:
                    self.wait_x(self.half(c, 1 - self.side, k), k)
                    self.c_copy(1 + k).start()
                else:
                    self.wait_x(self.half(c, lax.rem(x + 2, XS), k), 2 + k)
            if self.classes == XS:
                self.c_copy(3).start()

        def wait_core(self):
            for k, part in enumerate(self.core_parts(1 - c)):
                rc(part, part, self.cs.at[k], self.cr.at[k], sib).wait_recv()

        def wait_sends(self):
            @pl.when(self.at_class)
            def _():
                @pl.loop(1, Z)
                def _(o):
                    self.z_copy(o).wait_send()

            for k in range(3):
                self.y_copy(k).wait_send()

        def wait_late_sends(self):
            for k in range(2 if self.classes == 2 else 4):
                self.x_copy(k).wait_send()
            for k in range(len(self.core_parts(c))):
                self.c_copy(k).wait_send()

    wide = Spread(wall, wz_send, wz_recv, wy_send, wy_recv, wx_send, wx_recv, wc_send, wc_recv)
    quads = Spread(sall, sz_send, sz_recv, sy_send, sy_recv, sx_send, sx_recv, sc_send, sc_recv)

    def unfold(first, second):
        even = jnp.where(left, first, pltpu.roll(second, 64, 1))
        odd = jnp.where(left, pltpu.roll(first, 64, 1), second)
        return even, odd

    loads[2].wait()

    @pl.when(wide.at_class)
    def _():
        for k in range(UP):
            number = 2 * (UP * group + k) - c
            rows = lax.broadcasted_iota(jnp.int32, (15, 4096), 0)
            for tile in range(2):
                only = jnp.where(rows == number + tile, wfull[...].astype(F32), 0.0)
                only = jnp.sum(only, axis=0, keepdims=True)
                for r in range(32):
                    wfold[tile, r:r + 1, :] = only[:, 128 * r:128 * r + 128]
            even, odd = unfold(wfold[0], wfold[1])
            wpair[pl.ds(0, 32, stride=2), :] = even
            wpair[pl.ds(1, 32, stride=2), :] = odd
            wall[c, wide.side, UP * group + k, z // XS] = wpair[...].astype(BF16)

    pl.semaphore_wait(barrier, Z + Y + XS - 2)

    def row_start(e, core):
        dest = (z + e) % Z
        return jnp.minimum((CHIP_PAIRS * dest + 7 * core) // 4, RT - 3) * TILE

    def a_copy(e):
        rows = pl.ds(pl.multiple_of(row_start(e, 1 - c), TILE), 3 * TILE)
        return rc(at_ref.at[rows], a_sib.at[e], a_send.at[e], a_recv.at[e], sib)

    c_copy = rc(cot_ref, c_sib, c_send, c_recv, sib)
    c_copy.start()
    a_copy(H).start()

    a_copy(H - 1).start()
    a_copy(H + 1).start()

    loads[0].wait()
    loads[1].wait()
    rc(c_sib, c_sib, c_send, c_recv, sib).wait_recv()

    def partial(e, slot):
        rc(a_sib.at[e], a_sib.at[e], a_send.at[e], a_recv.at[e], sib).wait_recv()
        start = row_start(e, c)
        rows = pl.ds(pl.multiple_of(start, TILE), 3 * TILE)
        total = dot(a_own[rows, :], c_own[...]) + dot(a_sib[e], c_sib[...])
        total = total * scale
        for j in range(4):
            prod[j] = total[:, 128 * j:128 * j + 128]
        first = CHIP_PAIRS * ((z + e) % Z) + 7 * c
        for p in range(PAIRS):
            pair = first + p
            row = pl.multiple_of((pair // 4) * TILE - start, TILE)
            own[slot, p] = prod[pair % 4, pl.ds(row, TILE), :]

    def p_copy(s, q):
        return rc(send_p.at[s, pl.ds(2 * q, 2)], got_p.at[s, pl.ds(2 * q, 2)],
                  rp_send.at[s, q], rp_recv.at[s, q], at_z(1))

    def m_copy(s, q):
        return rc(send_m.at[s, pl.ds(2 * q, 2)], got_m.at[s, pl.ds(2 * q, 2)],
                  rm_send.at[s, q], rm_recv.at[s, q], at_z(Z - 1))

    partial(H, 0)
    for k in range(2):
        send_p[0, 2 * k:2 * k + 2] = own[0, 2 * k:2 * k + 2].astype(BF16)
        p_copy(0, k).start()
        send_m[0, 2 * k + 4:2 * k + 6] = own[0, 2 * k + 4:2 * k + 6].astype(BF16)
        m_copy(0, k + 2).start()

    @pl.loop(2, H)
    def _(s):
        a_copy(H - s).start()
        a_copy(H + s).start()

    a_copy(0).start()
    partial(H - 1, 2)
    partial(H + 1, 3)

    wide.start_z()

    @pl.loop(1, H)
    def _(s):
        now, later = 2 * (s % 2), 2 * ((s + 1) % 2)

        def pass_on(copy, got, send, slot, q, first):
            @pl.when(jnp.logical_or(s > 1, first))
            def _():
                copy(s - 1, q).wait_recv()

            part = own[slot, 2 * q:2 * q + 2] + got[s - 1, 2 * q:2 * q + 2].astype(F32)
            send[s, 2 * q:2 * q + 2] = part.astype(BF16)
            copy(s, q).start()

        for k in range(4):
            pass_on(p_copy, got_p, send_p, now, k, k < 2)
            pass_on(m_copy, got_m, send_m, now + 1, (k + 2) % 4, k < 2)
            if k == 1:
                partial(H - 1 - s, later)

        @pl.when(s < H - 1)
        def _():
            partial(H + 1 + s, later + 1)

        @pl.when(s == min(2, H - 1))
        def _():
            wide.wait_z()
            wide.start_y()

    last = 2 * (H % 2)

    loads[3].wait()
    loads[5].wait()
    loads[8].wait()
    loads[9].wait()
    for p in range(PAIRS):
        even, odd = unfold(mfold[1 + 2 * p - c], mfold[2 + 2 * p - c])
        u0[p, pl.ds(0, 32, stride=2), :] = even * momentum_decay
        u0[p, pl.ds(1, 32, stride=2), :] = odd * momentum_decay
    for p in range(PAIRS):
        u0[p] = own[last, p] + u0[p]
    high, rest = split(jnp.concatenate([u0[p] for p in range(PAIRS)], axis=1))
    side_own = dot(fine_ref[0:64, 0:64], high)
    side_own = side_own[0:32] + side_own[32:64] + dot(fine_ref[0:32, 0:64], rest)

    shape = (PAIRS * KEEP, 128)
    number = 2 * (lax.broadcasted_iota(jnp.int32, shape, 0) // KEEP) - c
    number = number + (lax.broadcasted_iota(jnp.int32, shape, 1) // KEEP) % 2
    keep = jnp.zeros(shape, F32)
    for s in range(8):
        listed = jnp.where(s < counts_ref[0, 0], chosen_ref[0, s], -5)
        keep = jnp.where(number == listed, 1.0, keep)

    wide.wait_y()
    wide.start_x()
    for q in range(4):
        p_copy(H - 1, q).wait_recv()
        m_copy(H - 1, q).wait_recv()
    arrived = jnp.concatenate(
        [jnp.concatenate([got[H - 1, p] for p in range(PAIRS)], axis=1) for got in (got_p, got_m)], axis=0)
    side = dot(fine_ref[0:64, :], arrived)
    side = side_own + (side[0:32] + side[32:64])
    side = jnp.concatenate([side[:, 128 * p:128 * p + 128] for p in range(PAIRS)], axis=0)
    high, rest = split(side)
    quad = dot(jnp.concatenate([high, rest, high], axis=1), fine_ref[128:512, :])
    quad = jnp.where(keep > 0.5, quad, 0.0).astype(BF16).astype(F32)
    odd_first = ((z + c) % 2) == 1
    for d in range(4):
        blocks = [quad[32 * p:32 * p + 32] for p in range(PAIRS)]
        plain = jnp.where(left, blocks[2 * d], blocks[2 * d + 1])
        turned = jnp.where(left, blocks[(2 * d + 7) % 8], blocks[2 * d])
        block = jnp.where(odd_first, turned, plain).astype(BF16)
        pack[2 * d] = block[0:16]
        pack[2 * d + 1] = block[16:32]

    def ry_copy(o):
        return rc(pack.at[pl.ds(UP * lax.rem(lax.rem(y + o, Y), 4), UP)], ys.at[o - 1],
                  ry_send.at[o - 1], ry_recv.at[o - 1], at_y(o))

    for o in far_first(Y):
        ry_copy(o).start()

    c_copy.wait_send()

    @pl.loop(0, Z)
    def _(e):
        a_copy(e).wait_send()

    for k in range(2):
        p_copy(0, k).wait_send()
        m_copy(0, k + 2).wait_send()

    @pl.loop(1, H)
    def _(s):
        for q in range(4):
            p_copy(s, q).wait_send()
            m_copy(s, q).wait_send()

    @pl.loop(1, Y)
    def _(o):
        ry_copy(o).wait_recv()

    total = pack[pl.ds(UP * group, UP)].astype(F32)
    for o in range(1, Y):
        total = total + ys[o - 1].astype(F32)
    xs[0] = total

    def rx_copy(o):
        return rc(xs.at[0], xs.at[o], rx_send.at[o - 1], rx_recv.at[o - 1], at_x(o))

    for o in far_first(XS):
        rx_copy(o).start()

    exact = quad.astype(BF16)
    quad_side = dot(jnp.concatenate([exact, exact], axis=1), fine_ref[512:768, :])
    quad_side = jnp.concatenate([quad_side[32 * p:32 * p + 32] for p in range(PAIRS)], axis=1)
    high, rest = split(quad_side)
    shift = dot(fine_ref[64:128, 0:96], jnp.concatenate([high, rest, high], axis=0))
    for p in range(PAIRS):
        got = got_p[H - 1, p].astype(F32) + got_m[H - 1, p].astype(F32)
        grad[p] = (u0[p] + got) - shift[:, 128 * p:128 * p + 128]

    for o in range(1, XS):
        rx_copy(o).wait_recv()
    total = (xs[0] + xs[2]) + (xs[1] + xs[3])

    @pl.when(quads.at_class)
    def _():
        for k in range(UP):
            sall[c, quads.side, UP * group + k, z // 2] = total[k].astype(BF16)

    quads.start_z()

    for p in range(PAIRS):
        even = grad[p, pl.ds(0, 32, stride=2), :]
        odd = grad[p, pl.ds(1, 32, stride=2), :]
        nfold[1 + 2 * p - c] = jnp.where(left, even, pltpu.roll(odd, 64, 1))
        nfold[2 + 2 * p - c] = jnp.where(left, pltpu.roll(even, 64, 1), odd)
    out_copy = pltpu.make_async_copy(nfold.at[pl.ds(1, 15)], newm_ref, out_sem)
    out_copy.start()

    @pl.loop(1, Y)
    def _(o):
        ry_copy(o).wait_send()

    for o in range(1, XS):
        rx_copy(o).wait_send()
    wide.wait_sends()
    wide.forward_x()
    quads.wait_z()
    quads.start_y()
    loads[4].wait()
    loads[6].wait()
    loads[7].wait()

    @pl.loop(0, KB)
    def _(k):
        rows = pl.ds(pl.multiple_of(256 * k, 256), 256)
        xr[:, rows] = xt[rows, :].T

    quads.wait_y()
    quads.start_x()
    wide.finish_x()

    @pl.loop(0, KB)
    def _(k):
        rows = pl.ds(pl.multiple_of(256 * k, 256), 256)
        low_in[:, pl.ds(pl.multiple_of(128 * k, 128), 128)] = dot(xr[:, rows], rl_ref[...]).astype(BF16)

    wide.wait_core()
    left64 = lax.broadcasted_iota(jnp.int32, (TILE, 128), 1) < 64
    for zz in range(Z):
        for p in range(CHIP_PAIRS):
            pair = CHIP_PAIRS * zz + p
            core, slot = (0, p) if p < 8 else (1, p - 7)
            block = wall[core, zz % XS, slot, zz // XS]
            if p == 7:
                block = jnp.where(left64, block, wall[1, zz % XS, 0, zz // XS])
            wmat[TILE * (pair // 4):TILE * (pair // 4) + TILE,
                 128 * (pair % 4):128 * (pair % 4) + 128] = block

    base[...] = jnp.zeros(base.shape, F32)

    @pl.loop(0, KB)
    def _(k):
        rows = pl.ds(pl.multiple_of(256 * k, 256), 256)
        base[...] += dot(xr[:, rows], wmat[rows, :])

    wide.wait_late_sends()
    quads.wait_sends()
    quads.finish_x()
    quads.wait_core()

    lane16 = lax.broadcasted_iota(jnp.int32, (16, 128), 1)
    for n, parts in enumerate(fold_sources(Z, D * 2 // 64)):
        for half in range(2):
            block = None
            for (core, zz, d), (lo, hi) in parts:
                part = sall[core, zz % 2, 2 * d + half, zz // 2]
                if block is None:
                    block = part
                else:
                    block = jnp.where((lane16 >= lo) & (lane16 < hi), part, block)
            row = 32 * (n // 2) + 16 * half
            smat[row:row + 16, 128 * (n % 2):128 * (n % 2) + 128] = block

    late = dot(low_in[...], smat[...]) * step_size
    values_ref[...] = (base[...] - dot(late.astype(BF16), cl_ref[...])).astype(BF16)

    out_copy.wait()
    quads.wait_late_sends()


def hand_over(values_ref, newm_ref, values_out, newm_out, values_here, newm_here, sems):
    moves = ((values_ref, values_here, values_out), (newm_ref, newm_here, newm_out))
    fetched = [pltpu.make_async_copy(a, b, sems.at[k]) for k, (a, b, _) in enumerate(moves)]
    stored = [pltpu.make_async_copy(b, d, sems.at[2 + k]) for k, (_, b, d) in enumerate(moves)]
    for copy in fetched:
        copy.start()
    for before, copy in zip(fetched, stored):
        before.wait()
        copy.start()
    for copy in stored:
        copy.wait()


def local(Y, Z, activations, cotangent, next_inputs, weight_tiles, momentum, chosen, counts):
    tokens, depth = activations.shape
    width = cotangent.shape[1]
    scale = 1.0 / math.sqrt(tokens * 2 * Z)
    H, UP = Z // 2, 2
    KB = -(-depth // 256)
    fine, rows_low, cols_low = tables(width // TILE)
    hbm = pl.BlockSpec(memory_space=pl.ANY)
    vmem = pl.BlockSpec(memory_space=pltpu.VMEM)
    dma = pltpu.SemaphoreType.DMA
    spread_sems = [dma((Z - 1,)), dma((Z // 2,)), dma((Y,)), dma((Y,)), dma((4,)), dma((4,)), dma((4,)), dma((4,))]
    pairs = (PAIRS, TILE, 128)
    scratch = [
        pltpu.VMEM((depth, tokens), BF16),
        pltpu.VMEM((tokens, width), BF16),
        pltpu.VMEM((Z, 3 * TILE, tokens), BF16),
        pltpu.VMEM((tokens, width), BF16),
        pltpu.VMEM((KB * 256, tokens), BF16),
        pltpu.VMEM((tokens, KB * 256), BF16),
        pltpu.VMEM((tokens, KB * 128), BF16),
        pltpu.VMEM((2, XS, PAIRS, Z // XS, TILE, 128), BF16),
        pltpu.VMEM((KB * 256, width), BF16),
        pltpu.VMEM((15, TILE * TILE), BF16),
        pltpu.VMEM((2, 32, 128), F32),
        pltpu.VMEM((17, 32, 128), F32),
        pltpu.VMEM((TILE, 128), F32),
        pltpu.VMEM(pairs, F32),
        pltpu.VMEM(pairs, F32),
        pltpu.VMEM((4, 3 * TILE, 128), F32),
        pltpu.VMEM((4,) + pairs, F32),
        pltpu.VMEM((H,) + pairs, BF16),
        pltpu.VMEM((H,) + pairs, BF16),
        pltpu.VMEM((H,) + pairs, BF16),
        pltpu.VMEM((H,) + pairs, BF16),
        pltpu.VMEM((8, 16, 128), BF16),
        pltpu.VMEM((Y, UP, 16, 128), BF16),
        pltpu.VMEM((XS, UP, 16, 128), F32),
        pltpu.VMEM((2, 2, PAIRS, Z // 2, 16, 128), BF16),
        pltpu.VMEM((KB * 128, width // 2), BF16),
        pltpu.VMEM((tokens, width), F32),
        pltpu.VMEM((17, 32, 128), F32),
        pltpu.VMEM(fine.shape, BF16),
        pltpu.VMEM(rows_low.shape, BF16),
        pltpu.VMEM(cols_low.shape, BF16),
        pltpu.SMEM((1, 8), jnp.int32),
        pltpu.SMEM((1, 1), jnp.int32),
        dma((10,)), dma((Z,)), dma((Z,)), dma(()), dma(()),
        dma((H, 4)), dma((H, 4)), dma((H, 4)), dma((H, 4)),
        *spread_sems, *spread_sems,
        dma((Y,)), dma((Y,)), dma((XS,)), dma((XS,)), dma(()),
    ]
    values, new_momentum = pl.pallas_call(
        functools.partial(kernel, Y, Z, scale),
        out_shape=(
            jax.ShapeDtypeStruct((tokens, width), BF16),
            jax.ShapeDtypeStruct((15, 32, 128), F32),
        ),
        in_specs=[hbm] * 10,
        out_specs=(vmem, hbm),
        scratch_shapes=scratch,
        compiler_params=pltpu.CompilerParams(
            collective_id=0, has_side_effects=True, vmem_limit_bytes=60 * 1024 * 1024),
        cost_estimate=pl.CostEstimate(
            flops=4 * tokens * depth * width, bytes_accessed=8 * tokens * depth, transcendentals=0),
    )(
        activations.T, cotangent, next_inputs.T, weight_tiles,
        momentum.reshape(15, 32, 128), chosen.reshape(1, 8), counts,
        jnp.asarray(fine), jnp.asarray(rows_low), jnp.asarray(cols_low),
    )
    values, new_momentum = pl.pallas_call(
        hand_over,
        out_shape=(
            jax.ShapeDtypeStruct(values.shape, values.dtype),
            jax.ShapeDtypeStruct(new_momentum.shape, new_momentum.dtype),
        ),
        in_specs=[hbm, hbm],
        out_specs=(hbm, hbm),
        scratch_shapes=[pltpu.VMEM(values.shape, BF16), pltpu.VMEM(new_momentum.shape, F32), dma((4,))],
        compiler_params=pltpu.CompilerParams(vmem_limit_bytes=60 * 1024 * 1024),
    )(values, new_momentum)
    return values, new_momentum.reshape(1, 15, TILE * TILE)


def solution(mesh):
    Y, Z = mesh.shape["replica"] // XS, mesh.shape["tok"] // 2
    return jax.shard_map(
        functools.partial(local, Y, Z),
        mesh=mesh,
        in_specs=(
            P(("replica", "tok"), None),
            P(("replica", "tok"), None),
            P(("replica", "tok"), None),
            P("tok", None),
            P("replica", "tok", None),
            P("replica", "tok", None),
            P("replica", "tok"),
        ),
        out_specs=(P(("replica", "tok"), None), P("replica", "tok", None)),
        check_vma=False,
    )
```
